128 devices in a mesh: blk: 16 (over x, y), sub: 8 (over z, core).
Axes of the slice: x: 4, y: 4, z: 4, core: 2. Of those that a mesh axis runs over, the one named last changes fastest.
Arguments:
- u_flow: float32 [16, 4096, 4096], P(None, 'blk', 'sub'), may hold values from -60 to 60
- v_flow: float32 [16, 4096, 4096], P(None, 'blk', 'sub'), may hold values from -60 to 60
- thickness: float32 [16], replicated, may hold values from 0.1 to 0.5
- depth_levels: int32 [4096, 4096], P('blk', 'sub'), may hold values from 1 to 16
- block_ocean: int32 [32, 32], replicated, may hold values from 0 to 1, as said below
- coef_x: float32 [4096, 4096], P('blk', 'sub'), may hold values from 0.2 to 1
- coef_y: float32 [4096, 4096], P('blk', 'sub'), may hold values from 0.2 to 1
- coef_xy: float32 [4096, 4096], P('blk', 'sub'), may hold values from 0.2 to 1
- coef_xm: float32 [4096, 4096], P('blk', 'sub'), may hold values from 0.2 to 1
- extra_diagonal: float32 [4096, 4096], P('blk', 'sub'), may hold values from 0.02 to 2
Outputs:
- surface_height: float32 [4096, 4096], P('blk', 'sub')
- residual: float32 [4096, 4096], P('blk', 'sub')
The draws below stay inside these ranges and needn't reach their ends.
Inputs may be any that keep to these rules, and one draw needn't show every extreme that they name: `block_ocean`: in every band of 256 rows of cells that one index of blk holds, exactly three quarters of the blocks are ocean blocks.
All inputs are finite; a program needn't handle non-finite values.
Results may differ from the reference program's by a relative error of at most 0.0003.
Values sent between devices are 32-bit elements; how exact they have to be, the bound alone decides.
A program may use at most 128 MiB of HBM per device.

```python
import math
import jax
import jax.numpy as jnp

BLOCK = 128
LEV = 16
ITERS = 4
CX = 256
NX = 4096
NY = 4096
NBX = 32
NBY = 32


def flow_field(seeded):
    rising = 1.0 + 2.0 * jnp.arange(NX, dtype=jnp.float32) / max(NX - 1, 1)
    values = jnp.clip(jax.random.normal(seeded, (LEV, NX, NY), jnp.float32), -5.0, 5.0)
    return values * rising[None, :, None]


def draw_u_flow(key, part):
    return flow_field(jax.random.fold_in(key, 11))


def draw_v_flow(key, part):
    return flow_field(jax.random.fold_in(key, 23))


def draw_block_ocean(key, part):
    band_rows = CX // BLOCK
    band_size = band_rows * NBY
    band_count = NBX // band_rows
    centre_x = jax.random.randint(jax.random.fold_in(key, 31), (6,), 0, NBX)
    centre_y = jax.random.randint(jax.random.fold_in(key, 37), (6,), 0, NBY)
    grid_x = jnp.arange(NBX, dtype=jnp.int32)[:, None, None]
    grid_y = jnp.arange(NBY, dtype=jnp.int32)[None, :, None]
    distance = jnp.min((grid_x - centre_x[None, None, :]) ** 2 + (grid_y - centre_y[None, None, :]) ** 2, axis=2)
    bands = distance.reshape(band_count, band_size)
    shuffle = jax.random.permutation(jax.random.fold_in(key, 41), band_size)
    shuffled = bands[:, shuffle]
    order = jnp.argsort(shuffled, axis=1, stable=True)
    chosen = shuffle[order[:, :band_size // 4]]
    band_index = jnp.arange(band_count, dtype=jnp.int32)[:, None] * jnp.ones((1, band_size // 4), jnp.int32)
    land = jnp.zeros((band_count, band_size), jnp.int32).at[band_index, chosen].set(1)
    return (1 - land).reshape(NBX, NBY).astype(jnp.int32)


def with_ends(array, rng, least, largest):
    extent = array.shape
    spot = [jax.random.randint(jax.random.fold_in(rng, axis), (), 0, extent[axis]) for axis in range(len(extent))]
    array = array.at[tuple(spot)].set(least)
    longest = extent.index(max(extent))
    spot[longest] = (spot[longest] + 1) % extent[longest]
    return array.at[tuple(spot)].set(largest)


def level_of(rng, dims, cuts, least, largest):
    def one(axis_at, shards_of):
        draws = jax.random.uniform(jax.random.fold_in(jax.random.fold_in(rng, 6), axis_at), (shards_of,), jnp.float32, least / len(cuts), largest / len(cuts))
        return jnp.repeat(jnp.exp(draws), dims[axis_at] // shards_of).reshape((-1,) + (1,) * (len(dims) - axis_at - 1))

    gain = one(*cuts[0])
    for cut in cuts[1:]:
        gain = gain * one(*cut)
    return gain


def setup_inputs(seed: int = 0) -> dict:
    key_of = jax.random.split(jax.random.key(seed), 11)
    u_flow = draw_u_flow(jax.random.fold_in(key_of[10], 71), 0)
    v_flow = draw_v_flow(jax.random.fold_in(key_of[10], 71), 0)
    thickness = jnp.clip(jnp.exp(jax.random.uniform(key_of[2], (LEV,), jnp.float32, math.log(0.1), math.log(0.5))), 0.1, 0.5)
    depth_levels = with_ends(jax.random.randint(key_of[3], (NX, NY), 1, LEV + 1), jax.random.fold_in(key_of[3], 1), 1, LEV).astype(jnp.int32)
    block_ocean = draw_block_ocean(jax.random.fold_in(key_of[10], 71), 0)
    coef_x = jnp.clip(0.2 + 0.8 * jax.random.uniform(key_of[5], (NX, NY), jnp.float32) ** level_of(key_of[5], (NX, NY), ((0, 16), (1, 8)), -0.2, 0.2), 0.2, 1.0)
    coef_y = jnp.clip(0.2 + 0.8 * jax.random.uniform(key_of[6], (NX, NY), jnp.float32) ** level_of(key_of[6], (NX, NY), ((0, 16), (1, 8)), -0.2, 0.2), 0.2, 1.0)
    coef_xy = jnp.clip(0.2 + 0.8 * jax.random.uniform(key_of[7], (NX, NY), jnp.float32) ** level_of(key_of[7], (NX, NY), ((0, 16), (1, 8)), -0.2, 0.2), 0.2, 1.0)
    coef_xm = jnp.clip(0.2 + 0.8 * jax.random.uniform(key_of[8], (NX, NY), jnp.float32) ** level_of(key_of[8], (NX, NY), ((0, 16), (1, 8)), -0.2, 0.2), 0.2, 1.0)
    extra_diagonal = jnp.clip(jnp.exp(math.log(2.0) - 4.6051702 * jax.random.uniform(key_of[9], (NX, NY), jnp.float32) ** level_of(key_of[9], (NX, NY), ((0, 16), (1, 8)), -0.2, 0.2)), 0.02, 2.0)
    return {"u_flow": u_flow, "v_flow": v_flow, "thickness": thickness, "depth_levels": depth_levels, "block_ocean": block_ocean, "coef_x": coef_x, "coef_y": coef_y, "coef_xy": coef_xy, "coef_xm": coef_xm, "extra_diagonal": extra_diagonal}


OFFSETS = ((1, 0), (-1, 0), (0, 1), (0, -1), (1, 1), (-1, -1), (1, -1), (-1, 1))


def shifted(field, offset_x, offset_y):
    padded = jnp.pad(field, 1)
    row_count, col_count = field.shape
    return padded[1 + offset_x:1 + offset_x + row_count, 1 + offset_y:1 + offset_y + col_count]


def reference(u_flow, v_flow, thickness, depth_levels, block_ocean, coef_x, coef_y, coef_xy, coef_xm, extra_diagonal):
    ocean_mask = jnp.repeat(jnp.repeat(block_ocean, BLOCK, axis=0), BLOCK, axis=1).astype(jnp.float32)
    flux_u = jnp.zeros(depth_levels.shape, jnp.float32)
    flux_v = jnp.zeros(depth_levels.shape, jnp.float32)
    for level_index in range(LEV):
        active = (depth_levels > level_index).astype(jnp.float32) * thickness[level_index]
        flux_u = flux_u + active * u_flow[level_index]
        flux_v = flux_v + active * v_flow[level_index]
    flux_u = ocean_mask * flux_u
    flux_v = ocean_mask * flux_v
    forcing = ocean_mask * (0.5 * ((shifted(flux_u, 1, 0) - shifted(flux_u, -1, 0)) + (shifted(flux_v, 0, 1) - shifted(flux_v, 0, -1))))
    weights = [coef_x, shifted(coef_x, -1, 0), coef_y, shifted(coef_y, 0, -1),
               coef_xy, shifted(coef_xy, -1, -1), coef_xm, shifted(coef_xm, -1, 1)]
    center = extra_diagonal
    for weight in weights:
        center = center + weight
    inverse = 1.0 / center

    def operate(field):
        beside = jnp.zeros(field.shape, jnp.float32)
        for offset, weight in zip(OFFSETS, weights):
            beside = beside + weight * shifted(field, offset[0], offset[1])
        return ocean_mask * (center * field - beside)

    surface_height = jnp.zeros(forcing.shape, jnp.float32)
    residual = forcing
    search = jnp.zeros(forcing.shape, jnp.float32)
    search_image = jnp.zeros(forcing.shape, jnp.float32)
    rho_old = jnp.float32(1.0)
    sigma_value = jnp.float32(0.0)
    for iteration in range(ITERS):
        scaled = residual * inverse
        applied = operate(scaled)
        rho_now = jnp.sum(residual * scaled)
        curvature = jnp.sum(scaled * applied)
        beta_ratio = rho_now / rho_old
        sigma_value = curvature - beta_ratio * beta_ratio * sigma_value
        alpha_step = rho_now / sigma_value
        rho_old = rho_now
        search = scaled + beta_ratio * search
        search_image = applied + beta_ratio * search_image
        surface_height = surface_height + alpha_step * search
        residual = residual - alpha_step * search_image
    return surface_height, residual
```

```python
import jax
import jax.numpy as jnp
from jax import lax
from jax.experimental import pallas as pl
from jax.experimental.pallas import tpu as pltpu
from jax.sharding import PartitionSpec as P

F32 = jnp.float32
LEV = 16
LANES = 128
MESH = pl.DeviceIdType.MESH


def column_mask(shape):
    return lax.broadcasted_iota(jnp.int32, shape, 1)


def kernel(u, v, th_hbm, depth_hbm, ocean_hbm, cx_hbm, cy_hbm, cxy_hbm, cxm_hbm, ex_hbm, height, residual,
           ub, vb, dp, th, ocean, co, fl, w, sh, cen, minv, out,
           pack_c, pack_f, in_c, in_f, corner_c, corner_f, sums, msg,
           small_sem, coef_sem, flow_sem, send_c, recv_c, send_f, recv_f, send_s, recv_s, out_sem, know_x, know_y):
    rows, cols = dp.shape
    slabs = cols // LANES
    halo = slabs
    top, first, last = 8, 16, 16 + rows
    nblk, nsub = lax.axis_size("blk"), lax.axis_size("sub")
    blk, sub = lax.axis_index("blk"), lax.axis_index("sub")
    n_all = nblk * nsub
    ring = 4

    small = [
        pltpu.make_async_copy(depth_hbm, dp, small_sem.at[0]),
        pltpu.make_async_copy(th_hbm, th, small_sem.at[1]),
        pltpu.make_async_copy(ocean_hbm, ocean, small_sem.at[2]),
    ]
    for copy in small:
        copy.start()
    flows = []

    def flow_copy(r0, r1, c0, c1):
        for src, dst in ((u, ub), (v, vb)):
            copy = pltpu.make_async_copy(src.at[:, r0:r1, c0:c1], dst.at[:, r0:r1, c0:c1], flow_sem.at[len(flows)])
            copy.start()
            flows.append(copy)
        return flows[-2:]

    strips = [flow_copy(0, 8, 0, cols), flow_copy(rows - 8, rows, 0, cols)]
    coefs = []
    for a, src in enumerate((cx_hbm, cy_hbm, cxy_hbm, cxm_hbm, ex_hbm)):
        for s in range(slabs):
            copy = pltpu.make_async_copy(
                src.at[:, s * LANES:(s + 1) * LANES], co.at[a, s, first:last, :], coef_sem.at[a, s])
            copy.start()
            coefs.append(copy)
    half = rows // 2
    quarters = [(8, half // 2), (half // 2, half), (half, half + half // 2), (half + half // 2, rows - 8)]
    outer = [[flow_copy(r0, r1, 0, LANES), flow_copy(r0, r1, cols - LANES, cols)] for r0, r1 in quarters]
    middle = [[flow_copy(r0, r1, LANES, cols - LANES)] for r0, r1 in quarters]

    def near(db, ds):
        return (lax.rem(blk + db + nblk, nblk), lax.rem(sub + ds + nsub, nsub))

    def along_x(d):
        return (lax.rem(blk // ring + d, ring) * ring + lax.rem(blk, ring), sub)

    def along_y(d):
        return ((blk // ring) * ring + lax.rem(lax.rem(blk, ring) + d, ring), sub)

    greeted = [near(db, ds) for db in (-1, 1) for ds in (-1, 0, 1)]
    greeted += [near(0, d) for d in range(1, 8)]
    greeted += [along_x(d) for d in range(1, ring)] + [along_y(d) for d in range(1, ring)]
    barrier = pltpu.get_barrier_semaphore()
    for device in greeted:
        pl.semaphore_signal(barrier, inc=1, device_id=device, device_id_type=MESH)

    lane = lax.broadcasted_iota(jnp.int32, (8, LANES), 1)
    left_ok = (sub > 0).astype(F32)
    right_ok = (sub < nsub - 1).astype(F32)
    up_ok = (blk > 0).astype(F32)
    down_ok = (blk < nblk - 1).astype(F32)
    low = lane < 64
    side_ok = jnp.where(low, right_ok, left_ok)

    for copy in small:
        copy.wait()

    def mask_at(a, s):
        row = blk * 2 + a
        col = sub * slabs + s
        ok = 1.0
        if a < 0:
            row, ok = jnp.maximum(row, 0), ok * up_ok
        if a > 1:
            row, ok = jnp.minimum(row, 2 * nblk - 1), ok * down_ok
        if s < 0:
            col, ok = jnp.maximum(col, 0), ok * left_ok
        if s >= slabs:
            col, ok = jnp.minimum(col, slabs * nsub - 1), ok * right_ok
        return ocean[row, col].astype(F32) * ok

    def column_sums(r0, r1, slab_list, block):
        masks = [mask_at(block, s) for s in slab_list]

        def tile(t, carry):
            base = pl.multiple_of(r0 + t * 8, 8)
            for s, mask in zip(slab_list, masks):
                at = pl.ds(s * LANES, LANES)
                deep = dp[pl.ds(base, 8), at]
                total_u = jnp.zeros((8, LANES), F32)
                total_v = jnp.zeros((8, LANES), F32)
                for k in range(LEV):
                    active = jnp.where(deep > k, th[k], 0.0)
                    total_u = total_u + active * ub[k, pl.ds(base, 8), at]
                    total_v = total_v + active * vb[k, pl.ds(base, 8), at]
                fl[0, s, pl.ds(first + base, 8), :] = mask * total_u
                fl[1, s, pl.ds(first + base, 8), :] = mask * total_v
            return carry

        lax.fori_loop(0, (r1 - r0) // 8, tile, 0)

    for (r0, block), copies in zip(((0, 0), (rows - 8, 1)), strips):
        for copy in copies:
            copy.wait()
        column_sums(r0, r0 + 8, range(slabs), block)

    def pack(field, n, packed):
        for side, s, shift in ((0, 0, 0), (1, slabs - 1, 8)):
            for a in range(n):
                for h in range(2):
                    total = jnp.zeros((8, LANES), F32)
                    for g in range(16):
                        value = field[a, s, first + 16 * g + 8 * h:first + 16 * g + 8 * h + 8, :]
                        turn = (8 * g + shift) % LANES
                        if turn:
                            value = pltpu.roll(value, turn, 1)
                        total = jnp.where(lane // 8 == g, value, total)
                    packed[side, a, 8 * h:8 * h + 8, :] = total

    def unpack(field, n, arrived, corners):
        for a in range(n):
            inside = (lambda factor: 1.0) if a == 4 else (lambda factor: factor)
            for h in range(2):
                ahead = arrived[0, a, 8 * h:8 * h + 8, :]
                behind = arrived[1, a, 8 * h:8 * h + 8, :]
                for g in range(16):
                    right, left = ahead, behind
                    if g:
                        right = pltpu.roll(ahead, LANES - 8 * g, 1)
                    if g < 15:
                        left = pltpu.roll(behind, 120 - 8 * g, 1)
                    field[a, halo, first + 16 * g + 8 * h:first + 16 * g + 8 * h + 8, :] = (
                        inside(side_ok) * jnp.where(low, right, left))
            for row, ok, (right, left) in ((top, up_ok, (2, 3)), (last, down_ok, (0, 1))):
                field[a, halo, row:row + 8, :] = inside(side_ok * ok) * jnp.where(low, corners[right, a], corners[left, a])
                for s in range(slabs):
                    field[a, s, row:row + 8, :] = inside(ok) * field[a, s, row:row + 8, :]

    def row_sends(field, corners, send, recv):
        made = []
        for way, db, src, dst in ((0, -1, first, last), (1, 1, last - 8, top)):
            made.append(pltpu.make_async_remote_copy(
                src_ref=field.at[:, 0:slabs, src:src + 8, :], dst_ref=field.at[:, 0:slabs, dst:dst + 8, :],
                send_sem=send.at[way], recv_sem=recv.at[way], device_id=near(db, 0), device_id_type=MESH))
            for side, ds, s in ((0, -1, 0), (1, 1, slabs - 1)):
                slot = 2 * way + side
                made.append(pltpu.make_async_remote_copy(
                    src_ref=field.at[:, s, src:src + 8, :], dst_ref=corners.at[slot],
                    send_sem=send.at[2 + slot], recv_sem=recv.at[2 + slot],
                    device_id=near(db, ds), device_id_type=MESH))
        return made

    def side_sends(packed, arrived, send, recv):
        return [pltpu.make_async_remote_copy(
            src_ref=packed.at[side], dst_ref=arrived.at[side], send_sem=send.at[6 + side], recv_sem=recv.at[6 + side],
            device_id=near(0, ds), device_id_type=MESH) for side, ds in ((0, -1), (1, 1))]

    for copy in coefs:
        copy.wait()
    pack(co, 5, pack_c)

    pl.semaphore_wait(barrier, len(greeted))
    flux_sends = row_sends(fl, corner_f, send_f, recv_f)
    coef_sends = row_sends(co, corner_c, send_c, recv_c) + side_sends(pack_c, in_c, send_c, recv_c)
    for copy in coef_sends + flux_sends:
        copy.start()
    for d in range(1, ring):
        pl.semaphore_signal(know_x, inc=1, device_id=along_x(d), device_id_type=MESH)

    for q, (r0, r1) in enumerate(quarters):
        for copies in outer[q]:
            for copy in copies:
                copy.wait()
        column_sums(r0, r1, (0, slabs - 1), q // 2)
    pack(fl, 2, pack_f)
    more = side_sends(pack_f, in_f, send_f, recv_f)
    for copy in more:
        copy.start()
    flux_sends += more

    for q, (r0, r1) in enumerate(quarters):
        for copies in middle[q]:
            for copy in copies:
                copy.wait()
        column_sums(r0, r1, range(1, slabs - 1), q // 2)

    pl.semaphore_wait(know_x, ring - 1)
    for d in range(1, ring):
        pl.semaphore_signal(know_y, inc=1, device_id=along_y(d), device_id_type=MESH)

    every = range(slabs + 1)

    def from_next(values):
        turned = [pltpu.roll(value, LANES - 1, 1) for value in values]
        return [jnp.where(lane == LANES - 1, turned[(s + 1) % len(values)], turned[s]) for s in range(len(values))]

    def from_before(values):
        turned = [pltpu.roll(value, 1, 1) for value in values]
        return [jnp.where(lane == 0, turned[s - 1], turned[s]) for s in range(len(values))]

    for copy in coef_sends:
        copy.wait()
    unpack(co, 5, in_c, corner_c)

    def shift_tile(t, carry):
        at = pl.ds(pl.multiple_of(top + t * 8, 8), 8)
        for a, (src, turn) in enumerate(((1, from_before), (2, from_before), (3, from_next))):
            for s, value in enumerate(turn([co[src, s, at, :] for s in every])):
                sh[a, s, at, :] = value
        return carry

    lax.fori_loop(0, rows // 8 + 2, shift_tile, 0)

    def centres(t0, t1, block):
        masks = [mask_at(block, s) for s in range(slabs)]
        masks.append(jnp.where(low, mask_at(block, slabs), mask_at(block, -1)))

        def tile(t, carry):
            base = pl.multiple_of(top + t * 8, 8)
            at, above = pl.ds(base, 8), pl.ds(base - 1, 8)
            for s in every:
                total = co[4, s, at, :] + co[0, s, at, :] + co[0, s, above, :]
                total = total + co[1, s, at, :] + sh[0, s, at, :]
                total = total + co[2, s, at, :] + sh[1, s, above, :]
                total = total + co[3, s, at, :] + sh[2, s, above, :]
                cen[s, at, :] = total
                minv[s, at, :] = masks[s] / total
            return carry

        lax.fori_loop(t0, t1, tile, 0)

    tiles = rows // 8
    centres(0, 1, -1)
    centres(1, 1 + tiles // 2, 0)
    centres(1 + tiles // 2, 1 + tiles, 1)
    centres(1 + tiles, 2 + tiles, 2)

    for copy in flux_sends:
        copy.wait()
    unpack(fl, 2, in_f, corner_f)

    def over_tiles(tile, count):
        tile(top, False)
        tile(last, False)

        def step(t, totals):
            more = tile(pl.multiple_of(first + t * 8, 8), True)
            return tuple(a + b for a, b in zip(totals, more))

        return lax.fori_loop(0, tiles, step, tuple(jnp.zeros((8, LANES), F32) for _ in range(count)))

    def dot(left, right):
        total = left[0] * right[0]
        for s in range(1, slabs):
            total = total + left[s] * right[s]
        return total

    def forcing_tile(base, own):
        at, above, below = pl.ds(base, 8), pl.ds(base - 1, 8), pl.ds(base + 1, 8)
        across = [fl[1, s, at, :] for s in every]
        ahead, behind = from_next(across), from_before(across)
        force, start = [], []
        for s in every:
            value = 0.5 * ((fl[0, s, below, :] - fl[0, s, above, :]) + (ahead[s] - behind[s]))
            force.append(value)
            start.append(minv[s, at, :] * value)
            w[0, s, at, :] = start[s]
        return (dot(force, start),)

    moments = list(over_tiles(forcing_tile, 1))

    def apply_tile(j, end):
        def tile(base, own):
            at, above, below = pl.ds(base, 8), pl.ds(base - 1, 8), pl.ds(base + 1, 8)
            ahead, behind, beside, here = [], [], [], []
            for s in every:
                up, mid, down = w[j, s, above, :], w[j, s, at, :], w[j, s, below, :]
                ahead.append(sh[0, s, at, :] * mid + sh[1, s, at, :] * down + co[3, s, above, :] * up)
                behind.append(co[1, s, at, :] * mid + co[2, s, above, :] * up + sh[2, s, at, :] * down)
                beside.append(co[0, s, at, :] * down + co[0, s, above, :] * up)
                here.append(mid)
            ahead, behind = from_next(ahead), from_before(behind)
            total, after = [], []
            for s in range(slabs if end else slabs + 1):
                total.append(beside[s] + ahead[s] + behind[s])
                after.append(minv[s, at, :] * total[s])
                w[j + 1, s, at, :] = after[s]
            if end:
                return (dot(total, here),)
            return (dot(total, here), dot(total, after))
        return tile

    for j in range(3):
        moments += over_tiles(apply_tile(j, False), 2)
    final = apply_tile(3, True)
    moments += lax.fori_loop(
        0, tiles, lambda t, totals: (totals[0] + final(pl.multiple_of(first + t * 8, 8), True)[0],),
        (jnp.zeros((8, LANES), F32),))

    line = jnp.zeros((1, LANES), F32)
    lane_1 = lax.broadcasted_iota(jnp.int32, (1, LANES), 1)
    for k, moment in enumerate(moments):
        number = jnp.sum(jnp.sum(moment, axis=0, keepdims=True), axis=1, keepdims=True)
        line = jnp.where(lane_1 == k, number, line)
    msg[...] = line
    pl.semaphore_wait(know_y, ring - 1)
    me = blk * nsub + sub

    def send(d, carry):
        other = lax.rem(me + d, n_all)
        pltpu.make_async_remote_copy(
            src_ref=msg, dst_ref=sums.at[d - 1], send_sem=send_s, recv_sem=recv_s,
            device_id=(other // nsub, lax.rem(other, nsub)), device_id_type=MESH).start()
        return carry

    lax.fori_loop(1, n_all, send, 0)
    whole = pltpu.make_async_remote_copy(
        src_ref=sums, dst_ref=sums, send_sem=send_s, recv_sem=recv_s, device_id=near(0, 1), device_id_type=MESH)
    whole.wait_recv()
    whole.wait_send()
    line = line + jnp.sum(sums[...], axis=0)
    m = [jnp.broadcast_to(line[:, k:k + 1], (8, LANES)) for k in range(8)]

    def inner(left, right):
        parts = [None] * (len(left) + len(right) - 1)
        for i, a in enumerate(left):
            for j, b in enumerate(right):
                parts[i + j] = a * b if parts[i + j] is None else parts[i + j] + a * b
        total = parts[0] * m[0]
        for k in range(1, len(parts)):
            total = total + parts[k] * m[k]
        return total

    def plus(left, factor, right):
        out_ = list(left)
        for i, b in enumerate(right):
            if i < len(out_):
                out_[i] = out_[i] + factor * b
            else:
                out_.append(factor * b)
        return out_

    one = jnp.ones((8, LANES), F32)
    res, search, image, high = [one], [], [], []
    rho_old = sigma = None
    for iteration in range(4):
        applied = plus(res + [jnp.zeros((8, LANES), F32)], -1.0, [jnp.zeros((8, LANES), F32)] + res)
        rho = inner(res, res)
        curvature = inner(res, applied)
        if iteration == 0:
            sigma, search, image = curvature, res, applied
        else:
            beta = rho / rho_old
            sigma = curvature - beta * beta * sigma
            search = plus(res, beta, search)
            image = plus(applied, beta, image)
        alpha = rho / sigma
        rho_old = rho
        high = plus(high, alpha, search)
        res = plus(res, -alpha, image)

    def combine(t, carry):
        base = pl.multiple_of(t * 8, 8)
        at = pl.ds(first + base, 8)
        for s in range(slabs):
            value = w[0, s, at, :]
            total_h, total_r = high[0] * value, res[0] * value
            for j in range(1, 4):
                value = w[j, s, at, :]
                total_h = total_h + high[j] * value
                total_r = total_r + res[j] * value
            total_r = total_r + res[4] * w[4, s, at, :]
            out[0, pl.ds(base, 8), s * LANES:(s + 1) * LANES] = total_h
            out[1, pl.ds(base, 8), s * LANES:(s + 1) * LANES] = total_r * cen[s, at, :]
        return carry

    ends = []
    for part in range(4):
        lax.fori_loop(part * tiles // 4, (part + 1) * tiles // 4, combine, 0)
        r0, r1 = part * rows // 4, (part + 1) * rows // 4
        for i, dst in enumerate((height, residual)):
            copy = pltpu.make_async_copy(out.at[i, r0:r1, :], dst.at[r0:r1, :], out_sem.at[part, i])
            copy.start()
            ends.append(copy)
    for copy in ends:
        copy.wait()


def body(*args):
    rows, cols = args[3].shape
    tall = rows + 32
    slabs = cols // LANES
    n_all = lax.axis_size("blk") * lax.axis_size("sub")
    any_ = pl.BlockSpec(memory_space=pl.ANY)
    dma = pltpu.SemaphoreType.DMA
    field = lambda *lead: pltpu.VMEM((*lead, slabs + 1, tall, LANES), F32)
    scratch = [
        pltpu.VMEM((LEV, rows, cols), F32), pltpu.VMEM((LEV, rows, cols), F32), pltpu.VMEM((rows, cols), jnp.int32),
        pltpu.SMEM((LEV,), F32), pltpu.SMEM(args[4].shape, jnp.int32),
        field(5), field(2), field(5), field(3), field(), field(), pltpu.VMEM((2, rows, cols), F32),
        pltpu.VMEM((2, 5, 16, LANES), F32), pltpu.VMEM((2, 2, 16, LANES), F32),
        pltpu.VMEM((2, 5, 16, LANES), F32), pltpu.VMEM((2, 2, 16, LANES), F32),
        pltpu.VMEM((4, 5, 8, LANES), F32), pltpu.VMEM((4, 2, 8, LANES), F32),
        pltpu.VMEM((n_all - 1, 1, LANES), F32), pltpu.VMEM((1, LANES), F32),
        dma((3,)), dma((5, slabs)), dma((28,)), dma((8,)), dma((8,)), dma((8,)), dma((8,)), dma, dma, dma((4, 2)),
        pltpu.SemaphoreType.REGULAR, pltpu.SemaphoreType.REGULAR,
    ]
    shape = jax.ShapeDtypeStruct((rows, cols), F32)
    return pl.pallas_call(
        kernel, out_shape=(shape, shape), in_specs=[any_] * 10, out_specs=(any_, any_), scratch_shapes=scratch,
        compiler_params=pltpu.CompilerParams(
            collective_id=0, has_side_effects=True, vmem_limit_bytes=56 * 1024 * 1024),
        cost_estimate=pl.CostEstimate(flops=20_000_000, bytes_accessed=20_000_000, transcendentals=0),
    )(*args)


def solution(mesh):
    tile = P("blk", "sub")
    flow = P(None, "blk", "sub")
    return jax.shard_map(
        body, mesh=mesh,
        in_specs=(flow, flow, P(), tile, P(), tile, tile, tile, tile, tile),
        out_specs=(tile, tile), check_vma=False)
```

```python
import jax
import jax.numpy as jnp
from jax import lax
from jax.experimental import pallas as pl
from jax.experimental.pallas import tpu as pltpu
from jax.sharding import PartitionSpec as P

F32 = jnp.float32
LEV = 16
LANES = 128
UNROLL = 8
MESH = pl.DeviceIdType.MESH


def column_mask(shape):
    return lax.broadcasted_iota(jnp.int32, shape, 1)


def kernel(u, v, th_hbm, depth_hbm, ocean_hbm, cx_hbm, cy_hbm, cxy_hbm, cxm_hbm, ex_hbm, w0, w1, w2, w3, w4, cen, mix,
           ub, vb, dp, th, ocean, co, fl, sh, minv,
           pack_c, pack_f, in_c, in_f, corner_c, corner_f, sums, msg,
           small_sem, coef_sem, flow_sem, send_c, recv_c, send_f, recv_f, send_s, recv_s, know_x, know_y):
    rows, cols = dp.shape
    slabs = cols // LANES
    halo = slabs
    top, first, last = 8, 16, 16 + rows
    nblk, nsub = lax.axis_size("blk"), lax.axis_size("sub")
    blk, sub = lax.axis_index("blk"), lax.axis_index("sub")
    ring = 4
    w = (w0, w1, w2, w3, w4)

    def near(db, ds):
        return (blk + db, sub + ds)

    def inside(db, ds):
        row, col = blk + db, sub + ds
        return (row >= 0) & (row < nblk) & (col >= 0) & (col < nsub)

    def on_sub(d):
        return (blk, lax.rem(sub + d, nsub))

    def along_x(d):
        return (lax.rem(blk // ring + d, ring) * ring + lax.rem(blk, ring), sub)

    def along_y(d):
        return ((blk // ring) * ring + lax.rem(lax.rem(blk, ring) + d, ring), sub)

    barrier = pltpu.get_barrier_semaphore()
    expected = 0
    for db in (-1, 1):
        for ds in (-1, 0, 1):
            there = inside(db, ds)
            expected = expected + there.astype(jnp.int32)

            @pl.when(there)
            def _(db=db, ds=ds):
                pl.semaphore_signal(barrier, inc=1, device_id=near(db, ds), device_id_type=MESH)

    greeted = [on_sub(d) for d in range(1, 8)]
    greeted += [along_x(d) for d in range(1, ring)] + [along_y(d) for d in range(1, ring)]
    for device in greeted:
        pl.semaphore_signal(barrier, inc=1, device_id=device, device_id_type=MESH)
    expected = expected + len(greeted)

    small = [
        pltpu.make_async_copy(depth_hbm, dp, small_sem.at[0]),
        pltpu.make_async_copy(th_hbm, th, small_sem.at[1]),
        pltpu.make_async_copy(ocean_hbm, ocean, small_sem.at[2]),
    ]
    for copy in small:
        copy.start()
    flows = []

    def flow_copy(r0, r1, c0, c1):
        for src, dst in ((u, ub), (v, vb)):
            copy = pltpu.make_async_copy(src.at[:, r0:r1, c0:c1], dst.at[:, r0:r1, c0:c1], flow_sem.at[len(flows)])
            copy.start()
            flows.append(copy)
        return flows[-2:]

    strips = [flow_copy(0, 8, 0, cols), flow_copy(rows - 8, rows, 0, cols)]
    coefs = []
    for a, src in enumerate((cx_hbm, cy_hbm, cxy_hbm, cxm_hbm, ex_hbm)):
        for s in range(slabs):
            copy = pltpu.make_async_copy(
                src.at[:, s * LANES:(s + 1) * LANES], co.at[a, s, first:last, :], coef_sem.at[a, s])
            copy.start()
            coefs.append(copy)
    half = rows // 2
    quarters = [(8, half // 2), (half // 2, half), (half, half + half // 2), (half + half // 2, rows - 8)]
    outer = [[flow_copy(r0, r1, 0, LANES), flow_copy(r0, r1, cols - LANES, cols)] for r0, r1 in quarters]
    middle = [[flow_copy(r0, r1, LANES, cols - LANES)] for r0, r1 in quarters]

    lane = lax.broadcasted_iota(jnp.int32, (8, LANES), 1)
    left_ok = (sub > 0).astype(F32)
    right_ok = (sub < nsub - 1).astype(F32)
    up_ok = (blk > 0).astype(F32)
    down_ok = (blk < nblk - 1).astype(F32)
    low = lane < 64
    side_in = jnp.where(low, right_ok, left_ok) > 0

    for copy in small:
        copy.wait()

    def mask_at(a, s):
        row = blk * 2 + a
        col = sub * slabs + s
        ok = 1.0
        if a < 0:
            row, ok = jnp.maximum(row, 0), ok * up_ok
        if a > 1:
            row, ok = jnp.minimum(row, 2 * nblk - 1), ok * down_ok
        if s < 0:
            col, ok = jnp.maximum(col, 0), ok * left_ok
        if s >= slabs:
            col, ok = jnp.minimum(col, slabs * nsub - 1), ok * right_ok
        return ocean[row, col].astype(F32) * ok

    def column_sums(r0, r1, slab_list, block):
        masks = [mask_at(block, s) for s in slab_list]

        def tile(t, carry):
            base = pl.multiple_of(r0 + t * 8, 8)
            for s, mask in zip(slab_list, masks):
                at = pl.ds(s * LANES, LANES)
                deep = dp[pl.ds(base, 8), at]
                total_u = jnp.zeros((8, LANES), F32)
                total_v = jnp.zeros((8, LANES), F32)
                for k in range(LEV):
                    active = jnp.where(deep > k, th[k], 0.0)
                    total_u = total_u + active * ub[k, pl.ds(base, 8), at]
                    total_v = total_v + active * vb[k, pl.ds(base, 8), at]
                fl[0, s, pl.ds(first + base, 8), :] = mask * total_u
                fl[1, s, pl.ds(first + base, 8), :] = mask * total_v
            return carry

        lax.fori_loop(0, (r1 - r0) // 8, tile, 0, unroll=min((r1 - r0) // 8, 2))

    for (r0, block), copies in zip(((0, 0), (rows - 8, 1)), strips):
        for copy in copies:
            copy.wait()
        column_sums(r0, r0 + 8, range(slabs), block)

    def pack(field, n, packed):
        for side, s, shift in ((0, 0, 0), (1, slabs - 1, 8)):
            for a in range(n):
                for h in range(2):
                    total = jnp.zeros((8, LANES), F32)
                    for g in range(16):
                        value = field[a, s, first + 16 * g + 8 * h:first + 16 * g + 8 * h + 8, :]
                        turn = (8 * g + shift) % LANES
                        if turn:
                            value = pltpu.roll(value, turn, 1)
                        total = jnp.where(lane // 8 == g, value, total)
                    packed[side, a, 8 * h:8 * h + 8, :] = total

    def unpack(field, n, arrived, corners):
        for a in range(n):
            outside = 1.0 if a == 4 else 0.0
            for h in range(2):
                ahead = arrived[0, a, 8 * h:8 * h + 8, :]
                behind = arrived[1, a, 8 * h:8 * h + 8, :]
                for g in range(16):
                    right, left = ahead, behind
                    if g:
                        right = pltpu.roll(ahead, LANES - 8 * g, 1)
                    if g < 15:
                        left = pltpu.roll(behind, 120 - 8 * g, 1)
                    field[a, halo, first + 16 * g + 8 * h:first + 16 * g + 8 * h + 8, :] = (
                        jnp.where(side_in, jnp.where(low, right, left), outside))
            for row, ok, (right, left) in ((top, up_ok, (2, 3)), (last, down_ok, (0, 1))):
                edge_in = jnp.broadcast_to(ok, lane.shape) > 0
                field[a, halo, row:row + 8, :] = jnp.where(
                    edge_in & side_in, jnp.where(low, corners[right, a], corners[left, a]), outside)
                for s in range(slabs):
                    field[a, s, row:row + 8, :] = jnp.where(edge_in, field[a, s, row:row + 8, :], outside)

    def row_sends(field, corners, send, recv):
        made = []
        for way, db, src, dst in ((0, -1, first, last), (1, 1, last - 8, top)):
            made.append(((db, 0), pltpu.make_async_remote_copy(
                src_ref=field.at[:, 0:slabs, src:src + 8, :], dst_ref=field.at[:, 0:slabs, dst:dst + 8, :],
                send_sem=send.at[way], recv_sem=recv.at[way], device_id=near(db, 0), device_id_type=MESH)))
            for side, ds, s in ((0, -1, 0), (1, 1, slabs - 1)):
                slot = 2 * way + side
                made.append(((db, ds), pltpu.make_async_remote_copy(
                    src_ref=field.at[:, s, src:src + 8, :], dst_ref=corners.at[slot],
                    send_sem=send.at[2 + slot], recv_sem=recv.at[2 + slot],
                    device_id=near(db, ds), device_id_type=MESH)))
        return made

    def side_sends(packed, arrived, send, recv):
        return [((0, ds), pltpu.make_async_remote_copy(
            src_ref=packed.at[side], dst_ref=arrived.at[side], send_sem=send.at[6 + side], recv_sem=recv.at[6 + side],
            device_id=near(0, ds), device_id_type=MESH)) for side, ds in ((0, -1), (1, 1))]

    def start_all(copies):
        for (db, ds), copy in copies:
            pl.when(inside(db, ds))(copy.start)

    def finish_all(copies):
        for (db, ds), copy in copies:
            pl.when(inside(-db, -ds))(copy.wait_recv)
            pl.when(inside(db, ds))(copy.wait_send)

    for copy in coefs:
        copy.wait()
    pack(co, 5, pack_c)

    pl.semaphore_wait(barrier, expected)
    flux_sends = row_sends(fl, corner_f, send_f, recv_f)
    coef_sends = row_sends(co, corner_c, send_c, recv_c) + side_sends(pack_c, in_c, send_c, recv_c)
    start_all(coef_sends + flux_sends)
    for d in range(1, ring):
        pl.semaphore_signal(know_x, inc=1, device_id=along_x(d), device_id_type=MESH)

    for q, (r0, r1) in enumerate(quarters):
        for copies in outer[q]:
            for copy in copies:
                copy.wait()
        column_sums(r0, r1, (0, slabs - 1), q // 2)
    pack(fl, 2, pack_f)
    more = side_sends(pack_f, in_f, send_f, recv_f)
    start_all(more)
    flux_sends += more

    for q, (r0, r1) in enumerate(quarters):
        for copies in middle[q]:
            for copy in copies:
                copy.wait()
        column_sums(r0, r1, range(1, slabs - 1), q // 2)

    pl.semaphore_wait(know_x, ring - 1)
    for d in range(1, ring):
        pl.semaphore_signal(know_y, inc=1, device_id=along_y(d), device_id_type=MESH)

    every = range(slabs + 1)

    def from_next(values):
        turned = [pltpu.roll(value, LANES - 1, 1) for value in values]
        return [jnp.where(lane == LANES - 1, turned[(s + 1) % len(values)], turned[s]) for s in range(len(values))]

    def from_before(values):
        turned = [pltpu.roll(value, 1, 1) for value in values]
        return [jnp.where(lane == 0, turned[s - 1], turned[s]) for s in range(len(values))]

    finish_all(coef_sends)
    unpack(co, 5, in_c, corner_c)

    def shift_tile(t, carry):
        at = pl.ds(pl.multiple_of(top + t * 8, 8), 8)
        for a, (src, turn) in enumerate(((1, from_before), (2, from_before), (3, from_next))):
            for s, value in enumerate(turn([co[src, s, at, :] for s in every])):
                sh[a, s, at, :] = value
        return carry

    lax.fori_loop(0, rows // 8 + 2, shift_tile, 0, unroll=2)

    def centres(t0, t1, block):
        masks = [mask_at(block, s) for s in range(slabs)]
        masks.append(jnp.where(low, mask_at(block, slabs), mask_at(block, -1)))

        def tile(t, carry):
            base = pl.multiple_of(top + t * 8, 8)
            at, above = pl.ds(base, 8), pl.ds(base - 1, 8)
            for s in every:
                total = co[4, s, at, :] + co[0, s, at, :] + co[0, s, above, :]
                total = total + co[1, s, at, :] + sh[0, s, at, :]
                total = total + co[2, s, at, :] + sh[1, s, above, :]
                total = total + co[3, s, at, :] + sh[2, s, above, :]
                cen[s, at, :] = total
                minv[s, at, :] = masks[s] / total
            return carry

        lax.fori_loop(t0, t1, tile, 0, unroll=min(t1 - t0, UNROLL))

    tiles = rows // 8
    centres(0, 1, -1)
    centres(1, 1 + tiles // 2, 0)
    centres(1 + tiles // 2, 1 + tiles, 1)
    centres(1 + tiles, 2 + tiles, 2)

    finish_all(flux_sends)
    unpack(fl, 2, in_f, corner_f)

    def over_tiles(tile, count):
        tile(top, False)
        tile(last, False)

        def step(t, totals):
            more = tile(pl.multiple_of(first + t * 8, 8), True)
            return tuple(a + b for a, b in zip(totals, more))

        return lax.fori_loop(0, tiles, step, tuple(jnp.zeros((8, LANES), F32) for _ in range(count)), unroll=UNROLL)

    def dot(left, right):
        total = left[0] * right[0]
        for s in range(1, slabs):
            total = total + left[s] * right[s]
        return total

    def forcing_tile(base, own):
        at, above, below = pl.ds(base, 8), pl.ds(base - 1, 8), pl.ds(base + 1, 8)
        across = [fl[1, s, at, :] for s in every]
        ahead, behind = from_next(across), from_before(across)
        force, start = [], []
        for s in every:
            value = 0.5 * ((fl[0, s, below, :] - fl[0, s, above, :]) + (ahead[s] - behind[s]))
            force.append(value)
            start.append(minv[s, at, :] * value)
            w[0][s, at, :] = start[s]
        return (dot(force, start),)

    moments = list(over_tiles(forcing_tile, 1))

    def apply_tile(j, end):
        def tile(base, own):
            at, above, below = pl.ds(base, 8), pl.ds(base - 1, 8), pl.ds(base + 1, 8)
            ahead, behind, beside, here = [], [], [], []
            for s in every:
                up, mid, down = w[j][s, above, :], w[j][s, at, :], w[j][s, below, :]
                ahead.append(sh[0, s, at, :] * mid + sh[1, s, at, :] * down + co[3, s, above, :] * up)
                behind.append(co[1, s, at, :] * mid + co[2, s, above, :] * up + sh[2, s, at, :] * down)
                beside.append(co[0, s, at, :] * down + co[0, s, above, :] * up)
                here.append(mid)
            ahead, behind = from_next(ahead), from_before(behind)
            total, after = [], []
            for s in range(slabs if end else slabs + 1):
                total.append(beside[s] + ahead[s] + behind[s])
                after.append(minv[s, at, :] * total[s])
                w[j + 1][s, at, :] = after[s]
            if end:
                return (dot(total, here),)
            return (dot(total, here), dot(total, after))
        return tile

    for j in range(3):
        moments += over_tiles(apply_tile(j, False), 2)
    final = apply_tile(3, True)
    moments += lax.fori_loop(
        0, tiles, lambda t, totals: (totals[0] + final(pl.multiple_of(first + t * 8, 8), True)[0],),
        (jnp.zeros((8, LANES), F32),), unroll=UNROLL)

    line = jnp.zeros((1, LANES), F32)
    lane_1 = lax.broadcasted_iota(jnp.int32, (1, LANES), 1)
    for k, moment in enumerate(moments):
        number = jnp.sum(jnp.sum(moment, axis=0, keepdims=True), axis=1, keepdims=True)
        line = jnp.where(lane_1 == k, number, line)
    msg[...] = line
    pl.semaphore_wait(know_y, ring - 1)
    x_at = [lax.rem(blk // ring + d, ring) * ring for d in range(ring)]
    y_at = [lax.rem(lax.rem(blk, ring) + d, ring) for d in range(ring)]
    sub_at = [lax.rem(sub + d, nsub) for d in range(8)]
    hops = (0, 1, 2, 1)
    ways = [(dx, dy, ds) for dx in range(ring) for dy in range(ring) for ds in range(8) if dx or dy or ds]
    ways.sort(key=lambda way: -hops[way[0]] - hops[way[1]] - hops[(way[2] + 1) // 2 % ring])
    for slot, (dx, dy, ds) in enumerate(ways):
        pltpu.make_async_remote_copy(
            src_ref=msg, dst_ref=sums.at[slot], send_sem=send_s, recv_sem=recv_s,
            device_id=(x_at[dx] + y_at[dy], sub_at[ds]), device_id_type=MESH).start()
    whole = pltpu.make_async_remote_copy(
        src_ref=sums, dst_ref=sums, send_sem=send_s, recv_sem=recv_s, device_id=on_sub(1), device_id_type=MESH)
    whole.wait_recv()
    whole.wait_send()
    line = line + jnp.sum(sums[...], axis=0)
    m = [jnp.broadcast_to(line[:, k:k + 1], (8, LANES)) for k in range(8)]

    def inner(left, right):
        parts = [None] * (len(left) + len(right) - 1)
        for i, a in enumerate(left):
            for j, b in enumerate(right):
                parts[i + j] = a * b if parts[i + j] is None else parts[i + j] + a * b
        total = parts[0] * m[0]
        for k in range(1, len(parts)):
            total = total + parts[k] * m[k]
        return total

    def plus(left, factor, right):
        out_ = list(left)
        for i, b in enumerate(right):
            if i < len(out_):
                out_[i] = out_[i] + factor * b
            else:
                out_.append(factor * b)
        return out_

    one = jnp.ones((8, LANES), F32)
    res, search, image, high = [one], [], [], []
    rho_old = sigma = None
    for iteration in range(4):
        applied = plus(res + [jnp.zeros((8, LANES), F32)], -1.0, [jnp.zeros((8, LANES), F32)] + res)
        rho = inner(res, res)
        curvature = inner(res, applied)
        if iteration == 0:
            sigma, search, image = curvature, res, applied
        else:
            beta = rho / rho_old
            sigma = curvature - beta * beta * sigma
            search = plus(res, beta, search)
            image = plus(applied, beta, image)
        alpha = rho / sigma
        rho_old = rho
        high = plus(high, alpha, search)
        res = plus(res, -alpha, image)

    for i, value in enumerate(high + res):
        mix[i] = value


def finish(w0, w1, w2, w3, w4, cen, mix, height, residual, out, out_sem):
    slabs, rows, first = cen.shape[0] - 1, out.shape[1], 16
    tiles = rows // 8
    high, res = [mix[i] for i in range(4)], [mix[4 + i] for i in range(5)]
    fields = (w0, w1, w2, w3, w4)

    def combine(t, carry):
        base = pl.multiple_of(t * 8, 8)
        at = pl.ds(first + base, 8)
        for s in range(slabs):
            value = fields[0][s, at, :]
            total_h, total_r = high[0] * value, res[0] * value
            for j in range(1, 4):
                value = fields[j][s, at, :]
                total_h = total_h + high[j] * value
                total_r = total_r + res[j] * value
            total_r = total_r + res[4] * fields[4][s, at, :]
            out[0, pl.ds(base, 8), s * LANES:(s + 1) * LANES] = total_h
            out[1, pl.ds(base, 8), s * LANES:(s + 1) * LANES] = total_r * cen[s, at, :]
        return carry

    ends = []
    for part in range(4):
        lax.fori_loop(part * tiles // 4, (part + 1) * tiles // 4, combine, 0, unroll=UNROLL)
        r0, r1 = part * rows // 4, (part + 1) * rows // 4
        for i, dst in enumerate((height, residual)):
            copy = pltpu.make_async_copy(out.at[i, r0:r1, :], dst.at[r0:r1, :], out_sem.at[part, i])
            copy.start()
            ends.append(copy)
    for copy in ends:
        copy.wait()


def body(*args):
    rows, cols = args[3].shape
    tall = rows + 32
    slabs = cols // LANES
    n_all = lax.axis_size("blk") * lax.axis_size("sub")
    any_ = pl.BlockSpec(memory_space=pl.ANY)
    dma = pltpu.SemaphoreType.DMA
    field = lambda *lead: pltpu.VMEM((*lead, slabs + 1, tall, LANES), F32)
    scratch = [
        pltpu.VMEM((LEV, rows, cols), F32), pltpu.VMEM((LEV, rows, cols), F32), pltpu.VMEM((rows, cols), jnp.int32),
        pltpu.SMEM((LEV,), F32), pltpu.SMEM(args[4].shape, jnp.int32),
        field(5), field(2), field(3), field(),
        pltpu.VMEM((2, 5, 16, LANES), F32), pltpu.VMEM((2, 2, 16, LANES), F32),
        pltpu.VMEM((2, 5, 16, LANES), F32), pltpu.VMEM((2, 2, 16, LANES), F32),
        pltpu.VMEM((4, 5, 8, LANES), F32), pltpu.VMEM((4, 2, 8, LANES), F32),
        pltpu.VMEM((n_all - 1, 1, LANES), F32), pltpu.VMEM((1, LANES), F32),
        dma((3,)), dma((5, slabs)), dma((28,)), dma((8,)), dma((8,)), dma((8,)), dma((8,)), dma, dma,
        pltpu.SemaphoreType.REGULAR, pltpu.SemaphoreType.REGULAR,
    ]
    vmem = pl.BlockSpec(memory_space=pltpu.VMEM)
    middle = pl.pallas_call(
        kernel, out_shape=[pltpu.VMEM((slabs + 1, tall, LANES), F32)] * 6 + [pltpu.VMEM((9, 8, LANES), F32)],
        in_specs=[pl.BlockSpec(memory_space=pltpu.HBM)] * 10, out_specs=[vmem] * 7, scratch_shapes=scratch,
        compiler_params=pltpu.CompilerParams(
            collective_id=0, has_side_effects=True, vmem_limit_bytes=59 * 1024 * 1024),
        cost_estimate=pl.CostEstimate(flops=20_000_000, bytes_accessed=20_000_000, transcendentals=0),
    )(*args)
    shape = jax.ShapeDtypeStruct((rows, cols), F32)
    return pl.pallas_call(
        finish, out_shape=(shape, shape), in_specs=[vmem] * 7, out_specs=(any_, any_),
        scratch_shapes=[pltpu.VMEM((2, rows, cols), F32), dma((4, 2))],
        compiler_params=pltpu.CompilerParams(vmem_limit_bytes=8 * 1024 * 1024),
        cost_estimate=pl.CostEstimate(flops=2_000_000, bytes_accessed=1_000_000, transcendentals=0),
    )(*middle)


def solution(mesh):
    tile = P("blk", "sub")
    flow = P(None, "blk", "sub")
    return jax.shard_map(
        body, mesh=mesh,
        in_specs=(flow, flow, P(), tile, P(), tile, tile, tile, tile, tile),
        out_specs=(tile, tile), check_vma=False)
```

```python
import jax
import jax.numpy as jnp
from jax import lax
from jax.experimental import pallas as pl
from jax.experimental.pallas import tpu as pltpu
from jax.sharding import PartitionSpec as P

F32 = jnp.float32
LEV = 16
LANES = 128
UNROLL = 8
MESH = pl.DeviceIdType.MESH


def column_mask(shape):
    return lax.broadcasted_iota(jnp.int32, shape, 1)


def kernel(u, v, th_hbm, depth_hbm, ocean_hbm, cx_hbm, cy_hbm, cxy_hbm, cxm_hbm, ex_hbm, w0, w1, w2, w3, w4, cen, mix,
           ub, vb, dp, th, ocean, co, fl, sh, minv,
           pack_c, pack_f, in_c, in_f, corner_c, corner_f, sums, msg,
           small_sem, coef_sem, flow_sem, send_c, recv_c, send_f, recv_f, send_s, recv_s, know_x, know_y):
    rows, cols = dp.shape
    slabs = cols // LANES
    halo = slabs
    top, first, last = 8, 16, 16 + rows
    nblk, nsub = lax.axis_size("blk"), lax.axis_size("sub")
    blk, sub = lax.axis_index("blk"), lax.axis_index("sub")
    ring = 4
    w = (w0, w1, w2, w3, w4)

    def near(db, ds):
        return (blk + db, sub + ds)

    def inside(db, ds):
        row, col = blk + db, sub + ds
        return (row >= 0) & (row < nblk) & (col >= 0) & (col < nsub)

    def on_sub(d):
        return (blk, lax.rem(sub + d, nsub))

    def along_x(d):
        return (lax.rem(blk // ring + d, ring) * ring + lax.rem(blk, ring), sub)

    def along_y(d):
        return ((blk // ring) * ring + lax.rem(lax.rem(blk, ring) + d, ring), sub)

    barrier = pltpu.get_barrier_semaphore()
    expected = 0
    for db in (-1, 1):
        for ds in (-1, 0, 1):
            there = inside(db, ds)
            expected = expected + there.astype(jnp.int32)

            @pl.when(there)
            def _(db=db, ds=ds):
                pl.semaphore_signal(barrier, inc=1, device_id=near(db, ds), device_id_type=MESH)

    greeted = [on_sub(d) for d in range(1, 8)]
    greeted += [along_x(d) for d in range(1, ring)] + [along_y(d) for d in range(1, ring)]
    for device in greeted:
        pl.semaphore_signal(barrier, inc=1, device_id=device, device_id_type=MESH)
    expected = expected + len(greeted)

    small = [
        pltpu.make_async_copy(depth_hbm, dp, small_sem.at[0]),
        pltpu.make_async_copy(th_hbm, th, small_sem.at[1]),
        pltpu.make_async_copy(ocean_hbm, ocean, small_sem.at[2]),
    ]
    for copy in small:
        copy.start()
    flows = []

    def flow_copy(r0, r1, c0, c1):
        for src, dst in ((u, ub), (v, vb)):
            copy = pltpu.make_async_copy(src.at[:, r0:r1, c0:c1], dst.at[:, r0:r1, c0:c1], flow_sem.at[len(flows)])
            copy.start()
            flows.append(copy)
        return flows[-2:]

    strips = [flow_copy(0, 8, 0, cols), flow_copy(rows - 8, rows, 0, cols)]
    coefs = []
    for a, src in enumerate((cx_hbm, cy_hbm, cxy_hbm, cxm_hbm, ex_hbm)):
        for s in range(slabs):
            copy = pltpu.make_async_copy(
                src.at[:, s * LANES:(s + 1) * LANES], co.at[a, s, first:last, :], coef_sem.at[a, s])
            copy.start()
            coefs.append(copy)
    half = rows // 2
    quarters = [(8, half // 2), (half // 2, half), (half, half + half // 2), (half + half // 2, rows - 8)]
    outer = [[flow_copy(r0, r1, 0, LANES), flow_copy(r0, r1, cols - LANES, cols)] for r0, r1 in quarters]
    middle = [[flow_copy(r0, r1, LANES, cols - LANES)] for r0, r1 in quarters]

    lane = lax.broadcasted_iota(jnp.int32, (8, LANES), 1)
    left_ok = (sub > 0).astype(F32)
    right_ok = (sub < nsub - 1).astype(F32)
    up_ok = (blk > 0).astype(F32)
    down_ok = (blk < nblk - 1).astype(F32)
    low = lane < 64
    side_in = jnp.where(low, right_ok, left_ok) > 0

    for copy in small:
        copy.wait()

    def mask_at(a, s):
        row = blk * 2 + a
        col = sub * slabs + s
        ok = 1.0
        if a < 0:
            row, ok = jnp.maximum(row, 0), ok * up_ok
        if a > 1:
            row, ok = jnp.minimum(row, 2 * nblk - 1), ok * down_ok
        if s < 0:
            col, ok = jnp.maximum(col, 0), ok * left_ok
        if s >= slabs:
            col, ok = jnp.minimum(col, slabs * nsub - 1), ok * right_ok
        return ocean[row, col].astype(F32) * ok

    def column_sums(r0, r1, slab_list, block):
        masks = [mask_at(block, s) for s in slab_list]

        def tile(t, carry):
            base = pl.multiple_of(r0 + t * 8, 8)
            for s, mask in zip(slab_list, masks):
                at = pl.ds(s * LANES, LANES)
                deep = dp[pl.ds(base, 8), at]
                total_u = jnp.zeros((8, LANES), F32)
                total_v = jnp.zeros((8, LANES), F32)
                for k in range(LEV):
                    active = jnp.where(deep > k, th[k], 0.0)
                    total_u = total_u + active * ub[k, pl.ds(base, 8), at]
                    total_v = total_v + active * vb[k, pl.ds(base, 8), at]
                fl[0, s, pl.ds(first + base, 8), :] = mask * total_u
                fl[1, s, pl.ds(first + base, 8), :] = mask * total_v
            return carry

        lax.fori_loop(0, (r1 - r0) // 8, tile, 0, unroll=min((r1 - r0) // 8, 2))

    for (r0, block), copies in zip(((0, 0), (rows - 8, 1)), strips):
        for copy in copies:
            copy.wait()
        column_sums(r0, r0 + 8, range(slabs), block)

    def pack(field, n, packed):
        for side, s, shift in ((0, 0, 0), (1, slabs - 1, 8)):
            for a in range(n):
                for h in range(2):
                    total = jnp.zeros((8, LANES), F32)
                    for g in range(16):
                        value = field[a, s, first + 16 * g + 8 * h:first + 16 * g + 8 * h + 8, :]
                        turn = (8 * g + shift) % LANES
                        if turn:
                            value = pltpu.roll(value, turn, 1)
                        total = jnp.where(lane // 8 == g, value, total)
                    packed[side, a, 8 * h:8 * h + 8, :] = total

    def unpack(field, n, arrived, corners):
        for a in range(n):
            outside = 1.0 if a == 4 else 0.0
            for h in range(2):
                ahead = arrived[0, a, 8 * h:8 * h + 8, :]
                behind = arrived[1, a, 8 * h:8 * h + 8, :]
                for g in range(16):
                    right, left = ahead, behind
                    if g:
                        right = pltpu.roll(ahead, LANES - 8 * g, 1)
                    if g < 15:
                        left = pltpu.roll(behind, 120 - 8 * g, 1)
                    field[a, halo, first + 16 * g + 8 * h:first + 16 * g + 8 * h + 8, :] = (
                        jnp.where(side_in, jnp.where(low, right, left), outside))
            for row, ok, (right, left) in ((top, up_ok, (2, 3)), (last, down_ok, (0, 1))):
                edge_in = jnp.broadcast_to(ok, lane.shape) > 0
                field[a, halo, row:row + 8, :] = jnp.where(
                    edge_in & side_in, jnp.where(low, corners[right, a], corners[left, a]), outside)
                for s in range(slabs):
                    field[a, s, row:row + 8, :] = jnp.where(edge_in, field[a, s, row:row + 8, :], outside)

    def row_sends(field, corners, send, recv):
        made = []
        for way, db, src, dst in ((0, -1, first, last), (1, 1, last - 8, top)):
            made.append(((db, 0), pltpu.make_async_remote_copy(
                src_ref=field.at[:, 0:slabs, src:src + 8, :], dst_ref=field.at[:, 0:slabs, dst:dst + 8, :],
                send_sem=send.at[way], recv_sem=recv.at[way], device_id=near(db, 0), device_id_type=MESH)))
            for side, ds, s in ((0, -1, 0), (1, 1, slabs - 1)):
                slot = 2 * way + side
                made.append(((db, ds), pltpu.make_async_remote_copy(
                    src_ref=field.at[:, s, src:src + 8, :], dst_ref=corners.at[slot],
                    send_sem=send.at[2 + slot], recv_sem=recv.at[2 + slot],
                    device_id=near(db, ds), device_id_type=MESH)))
        return made

    def side_sends(packed, arrived, send, recv):
        return [((0, ds), pltpu.make_async_remote_copy(
            src_ref=packed.at[side], dst_ref=arrived.at[side], send_sem=send.at[6 + side], recv_sem=recv.at[6 + side],
            device_id=near(0, ds), device_id_type=MESH)) for side, ds in ((0, -1), (1, 1))]

    def start_all(copies):
        for (db, ds), copy in copies:
            pl.when(inside(db, ds))(copy.start)

    def finish_all(copies):
        for (db, ds), copy in copies:
            pl.when(inside(-db, -ds))(copy.wait_recv)
            pl.when(inside(db, ds))(copy.wait_send)

    for copy in coefs:
        copy.wait()
    pack(co, 5, pack_c)

    pl.semaphore_wait(barrier, expected)
    flux_sends = row_sends(fl, corner_f, send_f, recv_f)
    coef_sends = row_sends(co, corner_c, send_c, recv_c) + side_sends(pack_c, in_c, send_c, recv_c)
    start_all(coef_sends + flux_sends)
    for d in range(1, ring):
        pl.semaphore_signal(know_x, inc=1, device_id=along_x(d), device_id_type=MESH)

    for q, (r0, r1) in enumerate(quarters):
        for copies in outer[q]:
            for copy in copies:
                copy.wait()
        column_sums(r0, r1, (0, slabs - 1), q // 2)
    pack(fl, 2, pack_f)
    more = side_sends(pack_f, in_f, send_f, recv_f)
    start_all(more)
    flux_sends += more

    every = range(slabs + 1)

    def from_next(values):
        turned = [pltpu.roll(value, LANES - 1, 1) for value in values]
        return [jnp.where(lane == LANES - 1, turned[(s + 1) % len(values)], turned[s]) for s in range(len(values))]

    def from_before(values):
        turned = [pltpu.roll(value, 1, 1) for value in values]
        return [jnp.where(lane == 0, turned[s - 1], turned[s]) for s in range(len(values))]

    def shift_own(t, carry):
        at = pl.ds(pl.multiple_of(first + t * 8, 8), 8)
        for a, (src, turn, rim) in enumerate(((1, 1, 0), (2, 1, 0), (3, LANES - 1, LANES - 1))):
            turned = [pltpu.roll(co[src, s, at, :], turn, 1) for s in range(slabs)]
            step = 1 if rim == 0 else -1
            for s in range(slabs):
                before = s - step
                sh[a, s, at, :] = jnp.where(lane == rim, turned[before], turned[s]) if 0 <= before < slabs else turned[s]
            sh[a, halo, at, :] = turned[slabs - 1 if rim == 0 else 0]
        return carry

    def shift_halo(at):
        for a, (src, turn, rim, edge) in enumerate(((1, 1, 0, 0), (2, 1, 0, 0), (3, LANES - 1, LANES - 1, slabs - 1))):
            turned = pltpu.roll(co[src, halo, at, :], turn, 1)
            sh[a, edge, at, :] = jnp.where(lane == rim, turned, sh[a, edge, at, :])
            sh[a, halo, at, :] = jnp.where(lane == rim, sh[a, halo, at, :], turned)

    def block_masks(block):
        return [mask_at(block, s) for s in range(slabs)] + [
            jnp.where(low, mask_at(block, slabs), mask_at(block, -1))]

    masks_0, masks_1 = block_masks(0), block_masks(1)

    def centre(base, slab_list, masks):
        at, above = pl.ds(base, 8), pl.ds(base - 1, 8)
        for s in slab_list:
            total = co[4, s, at, :] + co[0, s, at, :] + co[0, s, above, :]
            total = total + co[1, s, at, :] + sh[0, s, at, :]
            total = total + co[2, s, at, :] + sh[1, s, above, :]
            total = total + co[3, s, at, :] + sh[2, s, above, :]
            cen[s, at, :] = total
            minv[s, at, :] = masks[s] / total

    def own_centres(t, carry):
        masks = [jnp.where(t < tiles // 2, a, b) for a, b in zip(masks_0, masks_1)]
        centre(pl.multiple_of(first + t * 8, 8), range(1, slabs - 1), masks)
        return carry

    tiles = rows // 8
    lax.fori_loop(0, tiles, shift_own, 0, unroll=UNROLL)
    lax.fori_loop(1, tiles, own_centres, 0, unroll=UNROLL)

    for q, (r0, r1) in enumerate(quarters):
        for copies in middle[q]:
            for copy in copies:
                copy.wait()
        column_sums(r0, r1, range(1, slabs - 1), q // 2)

    pl.semaphore_wait(know_x, ring - 1)
    for d in range(1, ring):
        pl.semaphore_signal(know_y, inc=1, device_id=along_y(d), device_id_type=MESH)

    finish_all(coef_sends)
    unpack(co, 5, in_c, corner_c)
    for edge in (top, last):
        shift_own((edge - first) // 8, 0)
        shift_halo(pl.ds(edge, 8))

    def late_shift(t, carry):
        shift_halo(pl.ds(pl.multiple_of(first + t * 8, 8), 8))
        return carry

    lax.fori_loop(0, tiles, late_shift, 0, unroll=UNROLL)
    centre(top, every, block_masks(-1))
    centre(first, every, masks_0)
    centre(last, every, block_masks(2))

    def late_centres(t, carry):
        masks = [jnp.where(t < tiles // 2, a, b) for a, b in zip(masks_0, masks_1)]
        centre(pl.multiple_of(first + t * 8, 8), (0, slabs - 1, halo), masks)
        return carry

    lax.fori_loop(1, tiles, late_centres, 0, unroll=UNROLL)

    finish_all(flux_sends)
    unpack(fl, 2, in_f, corner_f)

    def over_tiles(tile, count):
        tile(top, False)
        tile(last, False)

        def step(t, totals):
            more = tile(pl.multiple_of(first + t * 8, 8), True)
            return tuple(a + b for a, b in zip(totals, more))

        return lax.fori_loop(0, tiles, step, tuple(jnp.zeros((8, LANES), F32) for _ in range(count)), unroll=UNROLL)

    def dot(left, right):
        total = left[0] * right[0]
        for s in range(1, slabs):
            total = total + left[s] * right[s]
        return total

    def forcing_tile(base, own):
        at, above, below = pl.ds(base, 8), pl.ds(base - 1, 8), pl.ds(base + 1, 8)
        across = [fl[1, s, at, :] for s in every]
        ahead, behind = from_next(across), from_before(across)
        force, start = [], []
        for s in every:
            value = 0.5 * ((fl[0, s, below, :] - fl[0, s, above, :]) + (ahead[s] - behind[s]))
            force.append(value)
            start.append(minv[s, at, :] * value)
            w[0][s, at, :] = start[s]
        return (dot(force, start),)

    moments = list(over_tiles(forcing_tile, 1))

    def apply_tile(j, end):
        def tile(base, own):
            at, above, below = pl.ds(base, 8), pl.ds(base - 1, 8), pl.ds(base + 1, 8)
            ahead, behind, beside, here = [], [], [], []
            for s in every:
                up, mid, down = w[j][s, above, :], w[j][s, at, :], w[j][s, below, :]
                ahead.append(sh[0, s, at, :] * mid + sh[1, s, at, :] * down + co[3, s, above, :] * up)
                behind.append(co[1, s, at, :] * mid + co[2, s, above, :] * up + sh[2, s, at, :] * down)
                beside.append(co[0, s, at, :] * down + co[0, s, above, :] * up)
                here.append(mid)
            ahead, behind = from_next(ahead), from_before(behind)
            total, after = [], []
            for s in range(slabs if end else slabs + 1):
                total.append(beside[s] + ahead[s] + behind[s])
                after.append(minv[s, at, :] * total[s])
                w[j + 1][s, at, :] = after[s]
            if end:
                return (dot(total, here),)
            return (dot(total, here), dot(total, after))
        return tile

    for j in range(3):
        moments += over_tiles(apply_tile(j, False), 2)
    final = apply_tile(3, True)
    moments += lax.fori_loop(
        0, tiles, lambda t, totals: (totals[0] + final(pl.multiple_of(first + t * 8, 8), True)[0],),
        (jnp.zeros((8, LANES), F32),), unroll=UNROLL)

    line = jnp.zeros((1, LANES), F32)
    lane_1 = lax.broadcasted_iota(jnp.int32, (1, LANES), 1)
    for k, moment in enumerate(moments):
        number = jnp.sum(jnp.sum(moment, axis=0, keepdims=True), axis=1, keepdims=True)
        line = jnp.where(lane_1 == k, number, line)
    msg[...] = line
    n_all = nblk * nsub
    sums[n_all - 1:n_all, :] = jnp.zeros((1, LANES), F32)
    pl.semaphore_wait(know_y, ring - 1)
    x_at = [lax.rem(blk // ring + d, ring) * ring for d in range(ring)]
    y_at = [lax.rem(lax.rem(blk, ring) + d, ring) for d in range(ring)]
    sub_at = [lax.rem(sub + d, nsub) for d in range(8)]
    hops = (0, 1, 2, 1)
    ways = [(dx, dy, ds) for dx in range(ring) for dy in range(ring) for ds in range(8) if dx or dy or ds]
    ways.sort(key=lambda way: -hops[way[0]] - hops[way[1]] - hops[(way[2] + 1) // 2 % ring])
    for slot, (dx, dy, ds) in enumerate(ways):
        pltpu.make_async_remote_copy(
            src_ref=msg, dst_ref=sums.at[slot:slot + 1, :], send_sem=send_s, recv_sem=recv_s,
            device_id=(x_at[dx] + y_at[dy], sub_at[ds]), device_id_type=MESH).start()
    whole = pltpu.make_async_remote_copy(
        src_ref=sums.at[0:n_all - 1, :], dst_ref=sums.at[0:n_all - 1, :], send_sem=send_s, recv_sem=recv_s, device_id=on_sub(1), device_id_type=MESH)
    whole.wait_recv()
    whole.wait_send()
    line = line + jnp.sum(sums[0:n_all, :], axis=0, keepdims=True)
    m = [jnp.broadcast_to(line[:, k:k + 1], (8, LANES)) for k in range(8)]

    def inner(left, right):
        parts = [None] * (len(left) + len(right) - 1)
        for i, a in enumerate(left):
            for j, b in enumerate(right):
                parts[i + j] = a * b if parts[i + j] is None else parts[i + j] + a * b
        total = parts[0] * m[0]
        for k in range(1, len(parts)):
            total = total + parts[k] * m[k]
        return total

    def plus(left, factor, right):
        out_ = list(left)
        for i, b in enumerate(right):
            if i < len(out_):
                out_[i] = out_[i] + factor * b
            else:
                out_.append(factor * b)
        return out_

    one = jnp.ones((8, LANES), F32)
    res, search, image, high = [one], [], [], []
    rho_old = sigma = None
    for iteration in range(4):
        applied = plus(res + [jnp.zeros((8, LANES), F32)], -1.0, [jnp.zeros((8, LANES), F32)] + res)
        rho = inner(res, res)
        curvature = inner(res, applied)
        if iteration == 0:
            sigma, search, image = curvature, res, applied
        else:
            beta = rho / rho_old
            sigma = curvature - beta * beta * sigma
            search = plus(res, beta, search)
            image = plus(applied, beta, image)
        alpha = rho / sigma
        rho_old = rho
        high = plus(high, alpha, search)
        res = plus(res, -alpha, image)

    for i, value in enumerate(high + res):
        mix[i] = value


def finish(w0, w1, w2, w3, w4, cen, mix, height, residual, out, out_sem):
    slabs, rows, first = cen.shape[0] - 1, out.shape[1], 16
    tiles = rows // 8
    high, res = [mix[i] for i in range(4)], [mix[4 + i] for i in range(5)]
    fields = (w0, w1, w2, w3, w4)

    def combine(t, carry):
        base = pl.multiple_of(t * 8, 8)
        at = pl.ds(first + base, 8)
        for s in range(slabs):
            value = fields[0][s, at, :]
            total_h, total_r = high[0] * value, res[0] * value
            for j in range(1, 4):
                value = fields[j][s, at, :]
                total_h = total_h + high[j] * value
                total_r = total_r + res[j] * value
            total_r = total_r + res[4] * fields[4][s, at, :]
            out[0, pl.ds(base, 8), s * LANES:(s + 1) * LANES] = total_h
            out[1, pl.ds(base, 8), s * LANES:(s + 1) * LANES] = total_r * cen[s, at, :]
        return carry

    ends = []
    for part in range(4):
        lax.fori_loop(part * tiles // 4, (part + 1) * tiles // 4, combine, 0, unroll=UNROLL)
        r0, r1 = part * rows // 4, (part + 1) * rows // 4
        for i, dst in enumerate((height, residual)):
            copy = pltpu.make_async_copy(out.at[i, r0:r1, :], dst.at[r0:r1, :], out_sem.at[part, i])
            copy.start()
            ends.append(copy)
    for copy in ends:
        copy.wait()


def body(*args):
    rows, cols = args[3].shape
    tall = rows + 32
    slabs = cols // LANES
    n_all = lax.axis_size("blk") * lax.axis_size("sub")
    any_ = pl.BlockSpec(memory_space=pl.ANY)
    dma = pltpu.SemaphoreType.DMA
    field = lambda *lead: pltpu.VMEM((*lead, slabs + 1, tall, LANES), F32)
    scratch = [
        pltpu.VMEM((LEV, rows, cols), F32), pltpu.VMEM((LEV, rows, cols), F32), pltpu.VMEM((rows, cols), jnp.int32),
        pltpu.SMEM((LEV,), F32), pltpu.SMEM(args[4].shape, jnp.int32),
        field(5), field(2), field(3), field(),
        pltpu.VMEM((2, 5, 16, LANES), F32), pltpu.VMEM((2, 2, 16, LANES), F32),
        pltpu.VMEM((2, 5, 16, LANES), F32), pltpu.VMEM((2, 2, 16, LANES), F32),
        pltpu.VMEM((4, 5, 8, LANES), F32), pltpu.VMEM((4, 2, 8, LANES), F32),
        pltpu.VMEM((n_all, LANES), F32), pltpu.VMEM((1, LANES), F32),
        dma((3,)), dma((5, slabs)), dma((28,)), dma((8,)), dma((8,)), dma((8,)), dma((8,)), dma, dma,
        pltpu.SemaphoreType.REGULAR, pltpu.SemaphoreType.REGULAR,
    ]
    vmem = pl.BlockSpec(memory_space=pltpu.VMEM)
    middle = pl.pallas_call(
        kernel, out_shape=[pltpu.VMEM((slabs + 1, tall, LANES), F32)] * 6 + [pltpu.VMEM((9, 8, LANES), F32)],
        in_specs=[pl.BlockSpec(memory_space=pltpu.HBM)] * 10, out_specs=[vmem] * 7, scratch_shapes=scratch,
        compiler_params=pltpu.CompilerParams(
            collective_id=0, has_side_effects=True, vmem_limit_bytes=59 * 1024 * 1024),
        cost_estimate=pl.CostEstimate(flops=20_000_000, bytes_accessed=20_000_000, transcendentals=0),
    )(*args)
    shape = jax.ShapeDtypeStruct((rows, cols), F32)
    return pl.pallas_call(
        finish, out_shape=(shape, shape), in_specs=[vmem] * 7, out_specs=(any_, any_),
        scratch_shapes=[pltpu.VMEM((2, rows, cols), F32), dma((4, 2))],
        compiler_params=pltpu.CompilerParams(vmem_limit_bytes=8 * 1024 * 1024),
        cost_estimate=pl.CostEstimate(flops=2_000_000, bytes_accessed=1_000_000, transcendentals=0),
    )(*middle)


def solution(mesh):
    tile = P("blk", "sub")
    flow = P(None, "blk", "sub")
    return jax.shard_map(
        body, mesh=mesh,
        in_specs=(flow, flow, P(), tile, P(), tile, tile, tile, tile, tile),
        out_specs=(tile, tile), check_vma=False)
```

```python
import jax
import jax.numpy as jnp
from jax import lax
from jax.experimental import pallas as pl
from jax.experimental.pallas import tpu as pltpu
from jax.sharding import PartitionSpec as P

F32 = jnp.float32
LEV = 16
LANES = 128
UNROLL = 8
MESH = pl.DeviceIdType.MESH


def column_mask(shape):
    return lax.broadcasted_iota(jnp.int32, shape, 1)


def kernel(u, v, th_hbm, depth_hbm, ocean_hbm, cx_hbm, cy_hbm, cxy_hbm, cxm_hbm, ex_hbm, w0, w1, w2, w3, w4, cen, mix,
           ub, vb, dp, th, ocean, co, fl, sh, minv,
           pack_c, pack_f, in_c, in_f, corner_c, corner_f, sums, msg,
           small_sem, coef_sem, flow_sem, send_c, recv_c, send_f, recv_f, send_s, recv_s, know_x, know_y):
    rows, cols = dp.shape
    slabs = cols // LANES
    halo = slabs
    top, first, last = 8, 16, 16 + rows
    nblk, nsub = lax.axis_size("blk"), lax.axis_size("sub")
    blk, sub = lax.axis_index("blk"), lax.axis_index("sub")
    ring = 4
    w = (w0, w1, w2, w3, w4)

    def near(db, ds):
        return (blk + db, sub + ds)

    def inside(db, ds):
        row, col = blk + db, sub + ds
        return (row >= 0) & (row < nblk) & (col >= 0) & (col < nsub)

    def on_sub(d):
        return (blk, lax.rem(sub + d, nsub))

    def along_x(d):
        return (lax.rem(blk // ring + d, ring) * ring + lax.rem(blk, ring), sub)

    def along_y(d):
        return ((blk // ring) * ring + lax.rem(lax.rem(blk, ring) + d, ring), sub)

    barrier = pltpu.get_barrier_semaphore()
    expected = 0
    for db in (-1, 1):
        for ds in (-1, 0, 1):
            there = inside(db, ds)
            expected = expected + there.astype(jnp.int32)

            @pl.when(there)
            def _(db=db, ds=ds):
                pl.semaphore_signal(barrier, inc=1, device_id=near(db, ds), device_id_type=MESH)

    greeted = [on_sub(d) for d in range(1, 8)]
    greeted += [along_x(d) for d in range(1, ring)] + [along_y(d) for d in range(1, ring)]
    for device in greeted:
        pl.semaphore_signal(barrier, inc=1, device_id=device, device_id_type=MESH)
    expected = expected + len(greeted)

    small = [
        pltpu.make_async_copy(depth_hbm, dp, small_sem.at[0]),
        pltpu.make_async_copy(th_hbm, th, small_sem.at[1]),
        pltpu.make_async_copy(ocean_hbm, ocean, small_sem.at[2]),
    ]
    for copy in small:
        copy.start()
    flows = []

    def flow_copy(r0, r1, c0, c1):
        for src, dst in ((u, ub), (v, vb)):
            copy = pltpu.make_async_copy(src.at[:, r0:r1, c0:c1], dst.at[:, r0:r1, c0:c1], flow_sem.at[len(flows)])
            copy.start()
            flows.append(copy)
        return flows[-2:]

    strips = [flow_copy(0, 8, 0, cols), flow_copy(rows - 8, rows, 0, cols)]
    coefs = []
    for a, src in enumerate((cx_hbm, cy_hbm, cxy_hbm, cxm_hbm, ex_hbm)):
        for s in range(slabs):
            copy = pltpu.make_async_copy(
                src.at[:, s * LANES:(s + 1) * LANES], co.at[a, s, first:last, :], coef_sem.at[a, s])
            copy.start()
            coefs.append(copy)
    half = rows // 2
    quarters = [(8, half // 2), (half // 2, half), (half, half + half // 2), (half + half // 2, rows - 8)]
    outer = [[flow_copy(r0, r1, 0, LANES), flow_copy(r0, r1, cols - LANES, cols)] for r0, r1 in quarters]
    middle = [[flow_copy(r0, r1, LANES, cols - LANES)] for r0, r1 in quarters]

    lane = lax.broadcasted_iota(jnp.int32, (8, LANES), 1)
    left_ok = (sub > 0).astype(F32)
    right_ok = (sub < nsub - 1).astype(F32)
    up_ok = (blk > 0).astype(F32)
    down_ok = (blk < nblk - 1).astype(F32)
    low = lane < 64
    side_in = jnp.where(low, right_ok, left_ok) > 0

    for copy in small:
        copy.wait()

    def mask_at(a, s):
        row = blk * 2 + a
        col = sub * slabs + s
        ok = 1.0
        if a < 0:
            row, ok = jnp.maximum(row, 0), ok * up_ok
        if a > 1:
            row, ok = jnp.minimum(row, 2 * nblk - 1), ok * down_ok
        if s < 0:
            col, ok = jnp.maximum(col, 0), ok * left_ok
        if s >= slabs:
            col, ok = jnp.minimum(col, slabs * nsub - 1), ok * right_ok
        return ocean[row, col].astype(F32) * ok

    def column_sums(r0, r1, slab_list, block):
        masks = [mask_at(block, s) for s in slab_list]

        def tile(t, carry):
            base = pl.multiple_of(r0 + t * 8, 8)
            for s, mask in zip(slab_list, masks):
                at = pl.ds(s * LANES, LANES)
                deep = dp[pl.ds(base, 8), at]
                total_u = jnp.zeros((8, LANES), F32)
                total_v = jnp.zeros((8, LANES), F32)
                for k in range(LEV):
                    active = jnp.where(deep > k, th[k], 0.0)
                    total_u = total_u + active * ub[k, pl.ds(base, 8), at]
                    total_v = total_v + active * vb[k, pl.ds(base, 8), at]
                fl[0, s, pl.ds(first + base, 8), :] = mask * total_u
                fl[1, s, pl.ds(first + base, 8), :] = mask * total_v
            return carry

        lax.fori_loop(0, (r1 - r0) // 8, tile, 0, unroll=min((r1 - r0) // 8, 2))

    for (r0, block), copies in zip(((0, 0), (rows - 8, 1)), strips):
        for copy in copies:
            copy.wait()
        column_sums(r0, r0 + 8, range(slabs), block)

    def pack(field, n, packed):
        for side, s, shift in ((0, 0, 0), (1, slabs - 1, 8)):
            for a in range(n):
                for h in range(2):
                    total = jnp.zeros((8, LANES), F32)
                    for g in range(16):
                        value = field[a, s, first + 16 * g + 8 * h:first + 16 * g + 8 * h + 8, :]
                        turn = (8 * g + shift) % LANES
                        if turn:
                            value = pltpu.roll(value, turn, 1)
                        total = jnp.where(lane // 8 == g, value, total)
                    packed[side, a, 8 * h:8 * h + 8, :] = total

    def unpack(field, n, arrived, corners):
        for a in range(n):
            outside = 1.0 if a == 4 else 0.0
            for h in range(2):
                ahead = arrived[0, a, 8 * h:8 * h + 8, :]
                behind = arrived[1, a, 8 * h:8 * h + 8, :]
                for g in range(16):
                    right, left = ahead, behind
                    if g:
                        right = pltpu.roll(ahead, LANES - 8 * g, 1)
                    if g < 15:
                        left = pltpu.roll(behind, 120 - 8 * g, 1)
                    field[a, halo, first + 16 * g + 8 * h:first + 16 * g + 8 * h + 8, :] = (
                        jnp.where(side_in, jnp.where(low, right, left), outside))
            for row, ok, (right, left) in ((top, up_ok, (2, 3)), (last, down_ok, (0, 1))):
                edge_in = jnp.broadcast_to(ok, lane.shape) > 0
                field[a, halo, row:row + 8, :] = jnp.where(
                    edge_in & side_in, jnp.where(low, corners[right, a], corners[left, a]), outside)
                for s in range(slabs):
                    field[a, s, row:row + 8, :] = jnp.where(edge_in, field[a, s, row:row + 8, :], outside)

    def row_sends(field, corners, send, recv):
        made = []
        for way, db, src, dst in ((0, -1, first, last), (1, 1, last - 8, top)):
            made.append(((db, 0), pltpu.make_async_remote_copy(
                src_ref=field.at[:, 0:slabs, src:src + 8, :], dst_ref=field.at[:, 0:slabs, dst:dst + 8, :],
                send_sem=send.at[way], recv_sem=recv.at[way], device_id=near(db, 0), device_id_type=MESH)))
            for side, ds, s in ((0, -1, 0), (1, 1, slabs - 1)):
                slot = 2 * way + side
                made.append(((db, ds), pltpu.make_async_remote_copy(
                    src_ref=field.at[:, s, src:src + 8, :], dst_ref=corners.at[slot],
                    send_sem=send.at[2 + slot], recv_sem=recv.at[2 + slot],
                    device_id=near(db, ds), device_id_type=MESH)))
        return made

    def side_sends(packed, arrived, send, recv):
        return [((0, ds), pltpu.make_async_remote_copy(
            src_ref=packed.at[side], dst_ref=arrived.at[side], send_sem=send.at[6 + side], recv_sem=recv.at[6 + side],
            device_id=near(0, ds), device_id_type=MESH)) for side, ds in ((0, -1), (1, 1))]

    def start_all(copies):
        for (db, ds), copy in copies:
            pl.when(inside(db, ds))(copy.start)

    def finish_all(copies):
        for (db, ds), copy in copies:
            pl.when(inside(-db, -ds))(copy.wait_recv)
            pl.when(inside(db, ds))(copy.wait_send)

    for copy in coefs:
        copy.wait()
    pack(co, 5, pack_c)

    pl.semaphore_wait(barrier, expected)
    flux_sends = row_sends(fl, corner_f, send_f, recv_f)
    coef_sends = row_sends(co, corner_c, send_c, recv_c) + side_sends(pack_c, in_c, send_c, recv_c)
    start_all(coef_sends + flux_sends)
    for d in range(1, ring):
        pl.semaphore_signal(know_x, inc=1, device_id=along_x(d), device_id_type=MESH)

    for q, (r0, r1) in enumerate(quarters):
        for copies in outer[q]:
            for copy in copies:
                copy.wait()
        column_sums(r0, r1, (0, slabs - 1), q // 2)
    pack(fl, 2, pack_f)
    more = side_sends(pack_f, in_f, send_f, recv_f)
    start_all(more)
    flux_sends += more

    every = range(slabs + 1)

    def from_next(values):
        turned = [pltpu.roll(value, LANES - 1, 1) for value in values]
        return [jnp.where(lane == LANES - 1, turned[(s + 1) % len(values)], turned[s]) for s in range(len(values))]

    def from_before(values):
        turned = [pltpu.roll(value, 1, 1) for value in values]
        return [jnp.where(lane == 0, turned[s - 1], turned[s]) for s in range(len(values))]

    def shift_own(t, carry):
        at = pl.ds(pl.multiple_of(first + t * 8, 8), 8)
        for a, (src, turn, rim) in enumerate(((1, 1, 0), (2, 1, 0), (3, LANES - 1, LANES - 1))):
            turned = [pltpu.roll(co[src, s, at, :], turn, 1) for s in range(slabs)]
            step = 1 if rim == 0 else -1
            for s in range(slabs):
                before = s - step
                sh[a, s, at, :] = jnp.where(lane == rim, turned[before], turned[s]) if 0 <= before < slabs else turned[s]
            sh[a, halo, at, :] = turned[slabs - 1 if rim == 0 else 0]
        return carry

    def shift_halo(at):
        for a, (src, turn, rim, edge) in enumerate(((1, 1, 0, 0), (2, 1, 0, 0), (3, LANES - 1, LANES - 1, slabs - 1))):
            turned = pltpu.roll(co[src, halo, at, :], turn, 1)
            sh[a, edge, at, :] = jnp.where(lane == rim, turned, sh[a, edge, at, :])
            sh[a, halo, at, :] = jnp.where(lane == rim, sh[a, halo, at, :], turned)

    def block_masks(block):
        return [mask_at(block, s) for s in range(slabs)] + [
            jnp.where(low, mask_at(block, slabs), mask_at(block, -1))]

    masks_0, masks_1 = block_masks(0), block_masks(1)

    def centre(base, slab_list, masks):
        at, above = pl.ds(base, 8), pl.ds(base - 1, 8)
        for s in slab_list:
            total = co[4, s, at, :] + co[0, s, at, :] + co[0, s, above, :]
            total = total + co[1, s, at, :] + sh[0, s, at, :]
            total = total + co[2, s, at, :] + sh[1, s, above, :]
            total = total + co[3, s, at, :] + sh[2, s, above, :]
            cen[s, at, :] = total
            minv[s, at, :] = masks[s] / total

    def own_centres(t, carry):
        masks = [jnp.where(t < tiles // 2, a, b) for a, b in zip(masks_0, masks_1)]
        centre(pl.multiple_of(first + t * 8, 8), range(1, slabs - 1), masks)
        return carry

    tiles = rows // 8
    lax.fori_loop(0, tiles, shift_own, 0, unroll=UNROLL)
    lax.fori_loop(1, tiles, own_centres, 0, unroll=UNROLL)

    for q, (r0, r1) in enumerate(quarters):
        for copies in middle[q]:
            for copy in copies:
                copy.wait()
        column_sums(r0, r1, range(1, slabs - 1), q // 2)

    pl.semaphore_wait(know_x, ring - 1)
    for d in range(1, ring):
        pl.semaphore_signal(know_y, inc=1, device_id=along_y(d), device_id_type=MESH)

    finish_all(coef_sends)
    unpack(co, 5, in_c, corner_c)
    for edge in (top, last):
        shift_own((edge - first) // 8, 0)
        shift_halo(pl.ds(edge, 8))

    def late_shift(t, carry):
        shift_halo(pl.ds(pl.multiple_of(first + t * 8, 8), 8))
        return carry

    lax.fori_loop(0, tiles, late_shift, 0, unroll=UNROLL)
    centre(top, every, block_masks(-1))
    centre(first, every, masks_0)
    centre(last, every, block_masks(2))

    def late_centres(t, carry):
        masks = [jnp.where(t < tiles // 2, a, b) for a, b in zip(masks_0, masks_1)]
        centre(pl.multiple_of(first + t * 8, 8), (0, slabs - 1, halo), masks)
        return carry

    lax.fori_loop(1, tiles, late_centres, 0, unroll=UNROLL)

    finish_all(flux_sends)
    unpack(fl, 2, in_f, corner_f)

    def over_tiles(tile, count):
        tile(top, False)
        tile(last, False)

        def step(t, totals):
            more = tile(pl.multiple_of(first + t * 8, 8), True)
            return tuple(a + b for a, b in zip(totals, more))

        return lax.fori_loop(0, tiles, step, tuple(jnp.zeros((8, LANES), F32) for _ in range(count)), unroll=tiles)

    def dot(left, right):
        total = left[0] * right[0]
        for s in range(1, slabs):
            total = total + left[s] * right[s]
        return total

    def forcing_tile(base, own):
        at, above, below = pl.ds(base, 8), pl.ds(base - 1, 8), pl.ds(base + 1, 8)
        across = [fl[1, s, at, :] for s in every]
        ahead, behind = from_next(across), from_before(across)
        force, start = [], []
        for s in every:
            value = 0.5 * ((fl[0, s, below, :] - fl[0, s, above, :]) + (ahead[s] - behind[s]))
            force.append(value)
            start.append(minv[s, at, :] * value)
            w[0][s, at, :] = start[s]
        return (dot(force, start),)

    moments = list(over_tiles(forcing_tile, 1))

    def apply_tile(j, end):
        def tile(base, own):
            at, above, below = pl.ds(base, 8), pl.ds(base - 1, 8), pl.ds(base + 1, 8)
            ahead, behind, beside, here = [], [], [], []
            for s in every:
                up, mid, down = w[j][s, above, :], w[j][s, at, :], w[j][s, below, :]
                ahead.append(sh[0, s, at, :] * mid + sh[1, s, at, :] * down + co[3, s, above, :] * up)
                behind.append(co[1, s, at, :] * mid + co[2, s, above, :] * up + sh[2, s, at, :] * down)
                beside.append(co[0, s, at, :] * down + co[0, s, above, :] * up)
                here.append(mid)
            ahead, behind = from_next(ahead), from_before(behind)
            total, after = [], []
            for s in range(slabs if end else slabs + 1):
                total.append(beside[s] + ahead[s] + behind[s])
                after.append(minv[s, at, :] * total[s])
                w[j + 1][s, at, :] = after[s]
            if end:
                return (dot(total, here),)
            return (dot(total, here), dot(total, after))
        return tile

    for j in range(3):
        moments += over_tiles(apply_tile(j, False), 2)
    final = apply_tile(3, True)
    moments += lax.fori_loop(
        0, tiles, lambda t, totals: (totals[0] + final(pl.multiple_of(first + t * 8, 8), True)[0],),
        (jnp.zeros((8, LANES), F32),), unroll=tiles)

    line = jnp.zeros((1, LANES), F32)
    lane_1 = lax.broadcasted_iota(jnp.int32, (1, LANES), 1)
    for k, moment in enumerate(moments):
        number = jnp.sum(jnp.sum(moment, axis=0, keepdims=True), axis=1, keepdims=True)
        line = jnp.where(lane_1 == k, number, line)
    msg[...] = line
    n_all = nblk * nsub
    sums[n_all - 1:n_all, :] = jnp.zeros((1, LANES), F32)
    pl.semaphore_wait(know_y, ring - 1)
    x_at = [lax.rem(blk // ring + d, ring) * ring for d in range(ring)]
    y_at = [lax.rem(lax.rem(blk, ring) + d, ring) for d in range(ring)]
    sub_at = [lax.rem(sub + d, nsub) for d in range(8)]
    hops = (0, 1, 2, 1)
    ways = [(dx, dy, ds) for dx in range(ring) for dy in range(ring) for ds in range(8) if dx or dy or ds]
    ways.sort(key=lambda way: -hops[way[0]] - hops[way[1]] - hops[(way[2] + 1) // 2 % ring])
    for slot, (dx, dy, ds) in enumerate(ways):
        pltpu.make_async_remote_copy(
            src_ref=msg, dst_ref=sums.at[slot:slot + 1, :], send_sem=send_s, recv_sem=recv_s,
            device_id=(x_at[dx] + y_at[dy], sub_at[ds]), device_id_type=MESH).start()
    whole = pltpu.make_async_remote_copy(
        src_ref=sums.at[0:n_all - 1, :], dst_ref=sums.at[0:n_all - 1, :], send_sem=send_s, recv_sem=recv_s, device_id=on_sub(1), device_id_type=MESH)
    whole.wait_recv()
    whole.wait_send()
    line = line + jnp.sum(sums[0:n_all, :], axis=0, keepdims=True)
    m = [jnp.broadcast_to(line[:, k:k + 1], (8, LANES)) for k in range(8)]

    def inner(left, right):
        parts = [None] * (len(left) + len(right) - 1)
        for i, a in enumerate(left):
            for j, b in enumerate(right):
                parts[i + j] = a * b if parts[i + j] is None else parts[i + j] + a * b
        total = parts[0] * m[0]
        for k in range(1, len(parts)):
            total = total + parts[k] * m[k]
        return total

    def plus(left, factor, right):
        out_ = list(left)
        for i, b in enumerate(right):
            if i < len(out_):
                out_[i] = out_[i] + factor * b
            else:
                out_.append(factor * b)
        return out_

    one = jnp.ones((8, LANES), F32)
    res, search, image, high = [one], [], [], []
    rho_old = sigma = None
    for iteration in range(4):
        applied = plus(res + [jnp.zeros((8, LANES), F32)], -1.0, [jnp.zeros((8, LANES), F32)] + res)
        rho = inner(res, res)
        curvature = inner(res, applied)
        if iteration == 0:
            sigma, search, image = curvature, res, applied
        else:
            beta = rho / rho_old
            sigma = curvature - beta * beta * sigma
            search = plus(res, beta, search)
            image = plus(applied, beta, image)
        alpha = rho / sigma
        rho_old = rho
        high = plus(high, alpha, search)
        res = plus(res, -alpha, image)

    for i, value in enumerate(high + res):
        mix[i] = value


def finish(w0, w1, w2, w3, w4, cen, mix, height, residual, out, out_sem):
    slabs, rows, first = cen.shape[0] - 1, out.shape[1], 16
    tiles = rows // 8
    high, res = [mix[i] for i in range(4)], [mix[4 + i] for i in range(5)]
    fields = (w0, w1, w2, w3, w4)

    def combine(t, carry):
        base = pl.multiple_of(t * 8, 8)
        at = pl.ds(first + base, 8)
        for s in range(slabs):
            value = fields[0][s, at, :]
            total_h, total_r = high[0] * value, res[0] * value
            for j in range(1, 4):
                value = fields[j][s, at, :]
                total_h = total_h + high[j] * value
                total_r = total_r + res[j] * value
            total_r = total_r + res[4] * fields[4][s, at, :]
            out[0, pl.ds(base, 8), s * LANES:(s + 1) * LANES] = total_h
            out[1, pl.ds(base, 8), s * LANES:(s + 1) * LANES] = total_r * cen[s, at, :]
        return carry

    ends = []
    for part in range(4):
        lax.fori_loop(part * tiles // 4, (part + 1) * tiles // 4, combine, 0, unroll=UNROLL)
        r0, r1 = part * rows // 4, (part + 1) * rows // 4
        for i, dst in enumerate((height, residual)):
            copy = pltpu.make_async_copy(out.at[i, r0:r1, :], dst.at[r0:r1, :], out_sem.at[part, i])
            copy.start()
            ends.append(copy)
    for copy in ends:
        copy.wait()


def body(*args):
    rows, cols = args[3].shape
    tall = rows + 32
    slabs = cols // LANES
    n_all = lax.axis_size("blk") * lax.axis_size("sub")
    any_ = pl.BlockSpec(memory_space=pl.ANY)
    dma = pltpu.SemaphoreType.DMA
    field = lambda *lead: pltpu.VMEM((*lead, slabs + 1, tall, LANES), F32)
    scratch = [
        pltpu.VMEM((LEV, rows, cols), F32), pltpu.VMEM((LEV, rows, cols), F32), pltpu.VMEM((rows, cols), jnp.int32),
        pltpu.SMEM((LEV,), F32), pltpu.SMEM(args[4].shape, jnp.int32),
        field(5), field(2), field(3), field(),
        pltpu.VMEM((2, 5, 16, LANES), F32), pltpu.VMEM((2, 2, 16, LANES), F32),
        pltpu.VMEM((2, 5, 16, LANES), F32), pltpu.VMEM((2, 2, 16, LANES), F32),
        pltpu.VMEM((4, 5, 8, LANES), F32), pltpu.VMEM((4, 2, 8, LANES), F32),
        pltpu.VMEM((n_all, LANES), F32), pltpu.VMEM((1, LANES), F32),
        dma((3,)), dma((5, slabs)), dma((28,)), dma((8,)), dma((8,)), dma((8,)), dma((8,)), dma, dma,
        pltpu.SemaphoreType.REGULAR, pltpu.SemaphoreType.REGULAR,
    ]
    vmem = pl.BlockSpec(memory_space=pltpu.VMEM)
    middle = pl.pallas_call(
        kernel, out_shape=[pltpu.VMEM((slabs + 1, tall, LANES), F32)] * 6 + [pltpu.VMEM((9, 8, LANES), F32)],
        in_specs=[pl.BlockSpec(memory_space=pltpu.HBM)] * 10, out_specs=[vmem] * 7, scratch_shapes=scratch,
        compiler_params=pltpu.CompilerParams(
            collective_id=0, has_side_effects=True, vmem_limit_bytes=59 * 1024 * 1024),
        cost_estimate=pl.CostEstimate(flops=20_000_000, bytes_accessed=20_000_000, transcendentals=0),
    )(*args)
    shape = jax.ShapeDtypeStruct((rows, cols), F32)
    return pl.pallas_call(
        finish, out_shape=(shape, shape), in_specs=[vmem] * 7, out_specs=(any_, any_),
        scratch_shapes=[pltpu.VMEM((2, rows, cols), F32), dma((4, 2))],
        compiler_params=pltpu.CompilerParams(vmem_limit_bytes=8 * 1024 * 1024),
        cost_estimate=pl.CostEstimate(flops=2_000_000, bytes_accessed=1_000_000, transcendentals=0),
    )(*middle)


def solution(mesh):
    tile = P("blk", "sub")
    flow = P(None, "blk", "sub")
    return jax.shard_map(
        body, mesh=mesh,
        in_specs=(flow, flow, P(), tile, P(), tile, tile, tile, tile, tile),
        out_specs=(tile, tile), check_vma=False)
```

```python
import jax
import jax.numpy as jnp
from jax import lax
from jax.experimental import pallas as pl
from jax.experimental.pallas import tpu as pltpu
from jax.sharding import PartitionSpec as P

F32 = jnp.float32
LEV = 16
LANES = 128
UNROLL = 8
MESH = pl.DeviceIdType.MESH


def column_mask(shape):
    return lax.broadcasted_iota(jnp.int32, shape, 1)


def kernel(u, v, th_hbm, depth_hbm, ocean_hbm, cx_hbm, cy_hbm, cxy_hbm, cxm_hbm, ex_hbm, w0, w1, w2, w3, w4, cen, mix,
           ub, vb, dp, th, ocean, co, fl, sh, minv,
           pack_c, pack_f, in_c, in_f, corner_c, corner_f, sums, msg,
           small_sem, coef_sem, flow_sem, send_c, recv_c, send_f, recv_f, send_s, recv_s, know_x, know_y):
    rows, cols = dp.shape
    slabs = cols // LANES
    halo = slabs
    top, first, last = 8, 16, 16 + rows
    nblk, nsub = lax.axis_size("blk"), lax.axis_size("sub")
    blk, sub = lax.axis_index("blk"), lax.axis_index("sub")
    ring = 4
    w = (w0, w1, w2, w3, w4)

    def near(db, ds):
        return (blk + db, sub + ds)

    def inside(db, ds):
        row, col = blk + db, sub + ds
        return (row >= 0) & (row < nblk) & (col >= 0) & (col < nsub)

    def on_sub(d):
        return (blk, lax.rem(sub + d, nsub))

    def along_x(d):
        return (lax.rem(blk // ring + d, ring) * ring + lax.rem(blk, ring), sub)

    def along_y(d):
        return ((blk // ring) * ring + lax.rem(lax.rem(blk, ring) + d, ring), sub)

    barrier = pltpu.get_barrier_semaphore()
    expected = 0
    for db in (-1, 1):
        for ds in (-1, 0, 1):
            there = inside(db, ds)
            expected = expected + there.astype(jnp.int32)

            @pl.when(there)
            def _(db=db, ds=ds):
                pl.semaphore_signal(barrier, inc=1, device_id=near(db, ds), device_id_type=MESH)

    greeted = [on_sub(d) for d in range(1, 8)]
    greeted += [along_x(d) for d in range(1, ring)] + [along_y(d) for d in range(1, ring)]
    for device in greeted:
        pl.semaphore_signal(barrier, inc=1, device_id=device, device_id_type=MESH)
    expected = expected + len(greeted)

    small = [
        pltpu.make_async_copy(depth_hbm, dp, small_sem.at[0]),
        pltpu.make_async_copy(th_hbm, th, small_sem.at[1]),
        pltpu.make_async_copy(ocean_hbm, ocean, small_sem.at[2]),
    ]
    for copy in small:
        copy.start()
    flows = []

    def flow_copy(r0, r1, c0, c1):
        for src, dst in ((u, ub), (v, vb)):
            copy = pltpu.make_async_copy(src.at[:, r0:r1, c0:c1], dst.at[:, r0:r1, c0:c1], flow_sem.at[len(flows)])
            copy.start()
            flows.append(copy)
        return flows[-2:]

    strips = [flow_copy(0, 8, 0, cols), flow_copy(rows - 8, rows, 0, cols)]
    coefs = []
    for a, src in enumerate((cx_hbm, cy_hbm, cxy_hbm, cxm_hbm, ex_hbm)):
        for s in range(slabs):
            copy = pltpu.make_async_copy(
                src.at[:, s * LANES:(s + 1) * LANES], co.at[a, s, first:last, :], coef_sem.at[a, s])
            copy.start()
            coefs.append(copy)
    half = rows // 2
    quarters = [(8, half // 2), (half // 2, half), (half, half + half // 2), (half + half // 2, rows - 8)]
    outer = [[flow_copy(r0, r1, 0, LANES), flow_copy(r0, r1, cols - LANES, cols)] for r0, r1 in quarters]
    middle = [[flow_copy(r0, r1, LANES, cols - LANES)] for r0, r1 in quarters]

    lane = lax.broadcasted_iota(jnp.int32, (8, LANES), 1)
    left_ok = (sub > 0).astype(F32)
    right_ok = (sub < nsub - 1).astype(F32)
    up_ok = (blk > 0).astype(F32)
    down_ok = (blk < nblk - 1).astype(F32)
    low = lane < 64
    side_in = jnp.where(low, right_ok, left_ok) > 0

    for copy in small:
        copy.wait()

    def mask_at(a, s):
        row = blk * 2 + a
        col = sub * slabs + s
        ok = 1.0
        if a < 0:
            row, ok = jnp.maximum(row, 0), ok * up_ok
        if a > 1:
            row, ok = jnp.minimum(row, 2 * nblk - 1), ok * down_ok
        if s < 0:
            col, ok = jnp.maximum(col, 0), ok * left_ok
        if s >= slabs:
            col, ok = jnp.minimum(col, slabs * nsub - 1), ok * right_ok
        return ocean[row, col].astype(F32) * ok

    def column_sums(r0, r1, slab_list, block):
        masks = [mask_at(block, s) for s in slab_list]

        def tile(t, carry):
            base = pl.multiple_of(r0 + t * 8, 8)
            for s, mask in zip(slab_list, masks):
                at = pl.ds(s * LANES, LANES)
                deep = dp[pl.ds(base, 8), at]
                total_u = jnp.zeros((8, LANES), F32)
                total_v = jnp.zeros((8, LANES), F32)
                for k in range(LEV):
                    active = jnp.where(deep > k, th[k], 0.0)
                    total_u = total_u + active * ub[k, pl.ds(base, 8), at]
                    total_v = total_v + active * vb[k, pl.ds(base, 8), at]
                fl[0, s, pl.ds(first + base, 8), :] = mask * total_u
                fl[1, s, pl.ds(first + base, 8), :] = mask * total_v
            return carry

        lax.fori_loop(0, (r1 - r0) // 8, tile, 0, unroll=min((r1 - r0) // 8, 2))

    for (r0, block), copies in zip(((0, 0), (rows - 8, 1)), strips):
        for copy in copies:
            copy.wait()
        column_sums(r0, r0 + 8, range(slabs), block)

    def pack(field, n, packed):
        for side, s, shift in ((0, 0, 0), (1, slabs - 1, 8)):
            for a in range(n):
                for h in range(2):
                    total = jnp.zeros((8, LANES), F32)
                    for g in range(16):
                        value = field[a, s, first + 16 * g + 8 * h:first + 16 * g + 8 * h + 8, :]
                        turn = (8 * g + shift) % LANES
                        if turn:
                            value = pltpu.roll(value, turn, 1)
                        total = jnp.where(lane // 8 == g, value, total)
                    packed[side, a, 8 * h:8 * h + 8, :] = total

    def unpack(field, n, arrived, corners):
        for a in range(n):
            outside = 1.0 if a == 4 else 0.0
            for h in range(2):
                ahead = arrived[0, a, 8 * h:8 * h + 8, :]
                behind = arrived[1, a, 8 * h:8 * h + 8, :]
                for g in range(16):
                    right, left = ahead, behind
                    if g:
                        right = pltpu.roll(ahead, LANES - 8 * g, 1)
                    if g < 15:
                        left = pltpu.roll(behind, 120 - 8 * g, 1)
                    field[a, halo, first + 16 * g + 8 * h:first + 16 * g + 8 * h + 8, :] = (
                        jnp.where(side_in, jnp.where(low, right, left), outside))
            for row, ok, (right, left) in ((top, up_ok, (2, 3)), (last, down_ok, (0, 1))):
                edge_in = jnp.broadcast_to(ok, lane.shape) > 0
                field[a, halo, row:row + 8, :] = jnp.where(
                    edge_in & side_in, jnp.where(low, corners[right, a], corners[left, a]), outside)
                for s in range(slabs):
                    field[a, s, row:row + 8, :] = jnp.where(edge_in, field[a, s, row:row + 8, :], outside)

    def row_sends(field, corners, send, recv):
        made = []
        for way, db, src, dst in ((0, -1, first, last), (1, 1, last - 8, top)):
            made.append(((db, 0), pltpu.make_async_remote_copy(
                src_ref=field.at[:, 0:slabs, src:src + 8, :], dst_ref=field.at[:, 0:slabs, dst:dst + 8, :],
                send_sem=send.at[way], recv_sem=recv.at[way], device_id=near(db, 0), device_id_type=MESH)))
            for side, ds, s in ((0, -1, 0), (1, 1, slabs - 1)):
                slot = 2 * way + side
                made.append(((db, ds), pltpu.make_async_remote_copy(
                    src_ref=field.at[:, s, src:src + 8, :], dst_ref=corners.at[slot],
                    send_sem=send.at[2 + slot], recv_sem=recv.at[2 + slot],
                    device_id=near(db, ds), device_id_type=MESH)))
        return made

    def side_sends(packed, arrived, send, recv):
        return [((0, ds), pltpu.make_async_remote_copy(
            src_ref=packed.at[side], dst_ref=arrived.at[side], send_sem=send.at[6 + side], recv_sem=recv.at[6 + side],
            device_id=near(0, ds), device_id_type=MESH)) for side, ds in ((0, -1), (1, 1))]

    def start_all(copies):
        for (db, ds), copy in copies:
            pl.when(inside(db, ds))(copy.start)

    def finish_all(copies):
        for (db, ds), copy in copies:
            pl.when(inside(-db, -ds))(copy.wait_recv)
            pl.when(inside(db, ds))(copy.wait_send)

    for copy in coefs:
        copy.wait()
    pack(co, 5, pack_c)

    pl.semaphore_wait(barrier, expected)
    flux_sends = row_sends(fl, corner_f, send_f, recv_f)
    coef_sends = row_sends(co, corner_c, send_c, recv_c) + side_sends(pack_c, in_c, send_c, recv_c)
    start_all(sorted(coef_sends, key=lambda entry: -abs(entry[0][0]) - abs(entry[0][1])) + sorted(flux_sends, key=lambda entry: -abs(entry[0][0]) - abs(entry[0][1])))
    for d in range(1, ring):
        pl.semaphore_signal(know_x, inc=1, device_id=along_x(d), device_id_type=MESH)

    for q, (r0, r1) in enumerate(quarters):
        for copies in outer[q]:
            for copy in copies:
                copy.wait()
        column_sums(r0, r1, (0, slabs - 1), q // 2)
    pack(fl, 2, pack_f)
    more = side_sends(pack_f, in_f, send_f, recv_f)
    start_all(more)
    flux_sends += more

    every = range(slabs + 1)

    def from_next(values):
        turned = [pltpu.roll(value, LANES - 1, 1) for value in values]
        return [jnp.where(lane == LANES - 1, turned[(s + 1) % len(values)], turned[s]) for s in range(len(values))]

    def from_before(values):
        turned = [pltpu.roll(value, 1, 1) for value in values]
        return [jnp.where(lane == 0, turned[s - 1], turned[s]) for s in range(len(values))]

    def shift_own(t, carry):
        at = pl.ds(pl.multiple_of(first + t * 8, 8), 8)
        for a, (src, turn, rim) in enumerate(((1, 1, 0), (2, 1, 0), (3, LANES - 1, LANES - 1))):
            turned = [pltpu.roll(co[src, s, at, :], turn, 1) for s in range(slabs)]
            step = 1 if rim == 0 else -1
            for s in range(slabs):
                before = s - step
                sh[a, s, at, :] = jnp.where(lane == rim, turned[before], turned[s]) if 0 <= before < slabs else turned[s]
            sh[a, halo, at, :] = turned[slabs - 1 if rim == 0 else 0]
        return carry

    def shift_halo(at):
        for a, (src, turn, rim, edge) in enumerate(((1, 1, 0, 0), (2, 1, 0, 0), (3, LANES - 1, LANES - 1, slabs - 1))):
            turned = pltpu.roll(co[src, halo, at, :], turn, 1)
            sh[a, edge, at, :] = jnp.where(lane == rim, turned, sh[a, edge, at, :])
            sh[a, halo, at, :] = jnp.where(lane == rim, sh[a, halo, at, :], turned)

    def block_masks(block):
        return [mask_at(block, s) for s in range(slabs)] + [
            jnp.where(low, mask_at(block, slabs), mask_at(block, -1))]

    masks_0, masks_1 = block_masks(0), block_masks(1)

    def centre(base, slab_list, masks):
        at, above = pl.ds(base, 8), pl.ds(base - 1, 8)
        for s in slab_list:
            total = co[4, s, at, :] + co[0, s, at, :] + co[0, s, above, :]
            total = total + co[1, s, at, :] + sh[0, s, at, :]
            total = total + co[2, s, at, :] + sh[1, s, above, :]
            total = total + co[3, s, at, :] + sh[2, s, above, :]
            cen[s, at, :] = total
            minv[s, at, :] = masks[s] / total

    def own_centres(t, carry):
        masks = [jnp.where(t < tiles // 2, a, b) for a, b in zip(masks_0, masks_1)]
        centre(pl.multiple_of(first + t * 8, 8), range(1, slabs - 1), masks)
        return carry

    tiles = rows // 8
    lax.fori_loop(0, tiles, shift_own, 0, unroll=UNROLL)
    lax.fori_loop(1, tiles, own_centres, 0, unroll=UNROLL)

    for q, (r0, r1) in enumerate(quarters):
        for copies in middle[q]:
            for copy in copies:
                copy.wait()
        column_sums(r0, r1, range(1, slabs - 1), q // 2)

    pl.semaphore_wait(know_x, ring - 1)
    for d in range(1, ring):
        pl.semaphore_signal(know_y, inc=1, device_id=along_y(d), device_id_type=MESH)

    finish_all(coef_sends)
    unpack(co, 5, in_c, corner_c)
    for edge in (top, last):
        shift_own((edge - first) // 8, 0)
        shift_halo(pl.ds(edge, 8))

    def late_shift(t, carry):
        shift_halo(pl.ds(pl.multiple_of(first + t * 8, 8), 8))
        return carry

    lax.fori_loop(0, tiles, late_shift, 0, unroll=UNROLL)
    centre(top, every, block_masks(-1))
    centre(first, every, masks_0)
    centre(last, every, block_masks(2))

    def late_centres(t, carry):
        masks = [jnp.where(t < tiles // 2, a, b) for a, b in zip(masks_0, masks_1)]
        centre(pl.multiple_of(first + t * 8, 8), (0, slabs - 1, halo), masks)
        return carry

    lax.fori_loop(1, tiles, late_centres, 0, unroll=UNROLL)

    finish_all(flux_sends)
    unpack(fl, 2, in_f, corner_f)

    def over_tiles(tile, count):
        tile(top, False)
        tile(last, False)

        def step(t, totals):
            more = tile(pl.multiple_of(first + t * 8, 8), True)
            return tuple(a + b for a, b in zip(totals, more))

        return lax.fori_loop(0, tiles, step, tuple(jnp.zeros((8, LANES), F32) for _ in range(count)), unroll=tiles)

    def dot(left, right):
        total = left[0] * right[0]
        for s in range(1, slabs):
            total = total + left[s] * right[s]
        return total

    def forcing_tile(base, own):
        at, above, below = pl.ds(base, 8), pl.ds(base - 1, 8), pl.ds(base + 1, 8)
        across = [fl[1, s, at, :] for s in every]
        ahead, behind = from_next(across), from_before(across)
        force, start = [], []
        for s in every:
            value = 0.5 * ((fl[0, s, below, :] - fl[0, s, above, :]) + (ahead[s] - behind[s]))
            force.append(value)
            start.append(minv[s, at, :] * value)
            w[0][s, at, :] = start[s]
        return (dot(force, start),)

    moments = list(over_tiles(forcing_tile, 1))

    def apply_tile(j, end):
        def tile(base, own):
            at, above, below = pl.ds(base, 8), pl.ds(base - 1, 8), pl.ds(base + 1, 8)
            ahead, behind, beside, here = [], [], [], []
            for s in every:
                up, mid, down = w[j][s, above, :], w[j][s, at, :], w[j][s, below, :]
                ahead.append(sh[0, s, at, :] * mid + sh[1, s, at, :] * down + co[3, s, above, :] * up)
                behind.append(co[1, s, at, :] * mid + co[2, s, above, :] * up + sh[2, s, at, :] * down)
                beside.append(co[0, s, at, :] * down + co[0, s, above, :] * up)
                here.append(mid)
            ahead, behind = from_next(ahead), from_before(behind)
            total, after = [], []
            for s in range(slabs if end else slabs + 1):
                total.append(beside[s] + ahead[s] + behind[s])
                after.append(minv[s, at, :] * total[s])
                w[j + 1][s, at, :] = after[s]
            if end:
                return (dot(total, here),)
            return (dot(total, here), dot(total, after))
        return tile

    for j in range(3):
        moments += over_tiles(apply_tile(j, False), 2)
    final = apply_tile(3, True)
    moments += lax.fori_loop(
        0, tiles, lambda t, totals: (totals[0] + final(pl.multiple_of(first + t * 8, 8), True)[0],),
        (jnp.zeros((8, LANES), F32),), unroll=tiles)

    line = jnp.zeros((1, LANES), F32)
    lane_1 = lax.broadcasted_iota(jnp.int32, (1, LANES), 1)
    for k, moment in enumerate(moments):
        number = jnp.sum(jnp.sum(moment, axis=0, keepdims=True), axis=1, keepdims=True)
        line = jnp.where(lane_1 == k, number, line)
    msg[...] = line
    n_all = nblk * nsub
    sums[n_all - 1:n_all, :] = jnp.zeros((1, LANES), F32)
    pl.semaphore_wait(know_y, ring - 1)
    x_at = [lax.rem(blk // ring + d, ring) * ring for d in range(ring)]
    y_at = [lax.rem(lax.rem(blk, ring) + d, ring) for d in range(ring)]
    sub_at = [lax.rem(sub + d, nsub) for d in range(8)]
    hops = (0, 1, 2, 1)
    ways = [(dx, dy, ds) for dx in range(ring) for dy in range(ring) for ds in range(8) if dx or dy or ds]
    ways.sort(key=lambda way: -hops[way[0]] - hops[way[1]] - hops[(way[2] + 1) // 2 % ring])
    for slot, (dx, dy, ds) in enumerate(ways):
        pltpu.make_async_remote_copy(
            src_ref=msg, dst_ref=sums.at[slot:slot + 1, :], send_sem=send_s, recv_sem=recv_s,
            device_id=(x_at[dx] + y_at[dy], sub_at[ds]), device_id_type=MESH).start()
    whole = pltpu.make_async_remote_copy(
        src_ref=sums.at[0:n_all - 1, :], dst_ref=sums.at[0:n_all - 1, :], send_sem=send_s, recv_sem=recv_s, device_id=on_sub(1), device_id_type=MESH)
    whole.wait_recv()
    whole.wait_send()
    line = line + jnp.sum(sums[0:n_all, :], axis=0, keepdims=True)
    m = [jnp.broadcast_to(line[:, k:k + 1], (8, LANES)) for k in range(8)]

    def inner(left, right):
        parts = [None] * (len(left) + len(right) - 1)
        for i, a in enumerate(left):
            for j, b in enumerate(right):
                parts[i + j] = a * b if parts[i + j] is None else parts[i + j] + a * b
        total = parts[0] * m[0]
        for k in range(1, len(parts)):
            total = total + parts[k] * m[k]
        return total

    def plus(left, factor, right):
        out_ = list(left)
        for i, b in enumerate(right):
            if i < len(out_):
                out_[i] = out_[i] + factor * b
            else:
                out_.append(factor * b)
        return out_

    one = jnp.ones((8, LANES), F32)
    res, search, image, high = [one], [], [], []
    rho_old = sigma = None
    for iteration in range(4):
        applied = plus(res + [jnp.zeros((8, LANES), F32)], -1.0, [jnp.zeros((8, LANES), F32)] + res)
        rho = inner(res, res)
        curvature = inner(res, applied)
        if iteration == 0:
            sigma, search, image = curvature, res, applied
        else:
            beta = rho / rho_old
            sigma = curvature - beta * beta * sigma
            search = plus(res, beta, search)
            image = plus(applied, beta, image)
        alpha = rho / sigma
        rho_old = rho
        high = plus(high, alpha, search)
        res = plus(res, -alpha, image)

    for i, value in enumerate(high + res):
        mix[i] = value


def finish(w0, w1, w2, w3, w4, cen, mix, height, residual, out, out_sem):
    slabs, rows, first = cen.shape[0] - 1, out.shape[1], 16
    tiles = rows // 8
    high, res = [mix[i] for i in range(4)], [mix[4 + i] for i in range(5)]
    fields = (w0, w1, w2, w3, w4)

    def combine(t, carry):
        base = pl.multiple_of(t * 8, 8)
        at = pl.ds(first + base, 8)
        for s in range(slabs):
            value = fields[0][s, at, :]
            total_h, total_r = high[0] * value, res[0] * value
            for j in range(1, 4):
                value = fields[j][s, at, :]
                total_h = total_h + high[j] * value
                total_r = total_r + res[j] * value
            total_r = total_r + res[4] * fields[4][s, at, :]
            out[0, pl.ds(base, 8), s * LANES:(s + 1) * LANES] = total_h
            out[1, pl.ds(base, 8), s * LANES:(s + 1) * LANES] = total_r * cen[s, at, :]
        return carry

    ends = []
    for part in range(4):
        lax.fori_loop(part * tiles // 4, (part + 1) * tiles // 4, combine, 0, unroll=UNROLL)
        r0, r1 = part * rows // 4, (part + 1) * rows // 4
        for i, dst in enumerate((height, residual)):
            copy = pltpu.make_async_copy(out.at[i, r0:r1, :], dst.at[r0:r1, :], out_sem.at[part, i])
            copy.start()
            ends.append(copy)
    for copy in ends:
        copy.wait()


def body(*args):
    rows, cols = args[3].shape
    tall = rows + 32
    slabs = cols // LANES
    n_all = lax.axis_size("blk") * lax.axis_size("sub")
    any_ = pl.BlockSpec(memory_space=pl.ANY)
    dma = pltpu.SemaphoreType.DMA
    field = lambda *lead: pltpu.VMEM((*lead, slabs + 1, tall, LANES), F32)
    scratch = [
        pltpu.VMEM((LEV, rows, cols), F32), pltpu.VMEM((LEV, rows, cols), F32), pltpu.VMEM((rows, cols), jnp.int32),
        pltpu.SMEM((LEV,), F32), pltpu.SMEM(args[4].shape, jnp.int32),
        field(5), field(2), field(3), field(),
        pltpu.VMEM((2, 5, 16, LANES), F32), pltpu.VMEM((2, 2, 16, LANES), F32),
        pltpu.VMEM((2, 5, 16, LANES), F32), pltpu.VMEM((2, 2, 16, LANES), F32),
        pltpu.VMEM((4, 5, 8, LANES), F32), pltpu.VMEM((4, 2, 8, LANES), F32),
        pltpu.VMEM((n_all, LANES), F32), pltpu.VMEM((1, LANES), F32),
        dma((3,)), dma((5, slabs)), dma((28,)), dma((8,)), dma((8,)), dma((8,)), dma((8,)), dma, dma,
        pltpu.SemaphoreType.REGULAR, pltpu.SemaphoreType.REGULAR,
    ]
    vmem = pl.BlockSpec(memory_space=pltpu.VMEM)
    middle = pl.pallas_call(
        kernel, out_shape=[pltpu.VMEM((slabs + 1, tall, LANES), F32)] * 6 + [pltpu.VMEM((9, 8, LANES), F32)],
        in_specs=[pl.BlockSpec(memory_space=pltpu.HBM)] * 10, out_specs=[vmem] * 7, scratch_shapes=scratch,
        compiler_params=pltpu.CompilerParams(
            collective_id=0, has_side_effects=True, vmem_limit_bytes=59 * 1024 * 1024),
        cost_estimate=pl.CostEstimate(flops=20_000_000, bytes_accessed=20_000_000, transcendentals=0),
    )(*args)
    shape = jax.ShapeDtypeStruct((rows, cols), F32)
    return pl.pallas_call(
        finish, out_shape=(shape, shape), in_specs=[vmem] * 7, out_specs=(any_, any_),
        scratch_shapes=[pltpu.VMEM((2, rows, cols), F32), dma((4, 2))],
        compiler_params=pltpu.CompilerParams(vmem_limit_bytes=8 * 1024 * 1024),
        cost_estimate=pl.CostEstimate(flops=2_000_000, bytes_accessed=1_000_000, transcendentals=0),
    )(*middle)


def solution(mesh):
    tile = P("blk", "sub")
    flow = P(None, "blk", "sub")
    return jax.shard_map(
        body, mesh=mesh,
        in_specs=(flow, flow, P(), tile, P(), tile, tile, tile, tile, tile),
        out_specs=(tile, tile), check_vma=False)
```
